512 devices in a mesh: row: 16 (over z), col: 32 (over x, y, core).
Axes of the slice: x: 4, y: 4, z: 16, core: 2. Of those that a mesh axis runs over, the one named last changes fastest.
Arguments:
- tensor: float32 [8, 2048, 8192], P(None, 'row', 'col'), may hold values from -12288 to 12288
- factor_b: float32 [256, 8192], P('row', 'col'), may hold values from -6 to 6
- factor_c: float32 [8, 256], replicated, may hold values from -6 to 6
Outputs:
- new_a: float32 [2048, 256], P(('row', 'col'))
- new_b: float32 [256, 8192], P('row', 'col')
- new_c: float32 [8, 256], replicated
The draws below stay inside these ranges and needn't reach their ends.
All inputs are finite; a program needn't handle non-finite values.
Results may differ from the reference program's by a relative error of at most 0.0001.
Values sent between devices are 32-bit elements; how exact they have to be, the bound alone decides.
A program may use at most 64 MiB of HBM per device.

```python
import jax
import jax.numpy as jnp
from jax import lax

R = 256
K = 8
J_DEV = 256
NI = 2048
NJ = 8192
N_COL = 32


def strengthened(entries, own_key, source, target, blocks, factor):
    def block_of(position):
        return (jnp.arange(entries.shape[position]) // (entries.shape[position] // blocks)).reshape((-1,) + (1,) * (entries.ndim - 1 - position))

    near = jax.random.permutation(own_key, blocks)[block_of(target)]
    second = (block_of(target) + blocks // 2) % blocks
    return jnp.where((block_of(source) == near) | (block_of(source) == second), factor * entries, entries)


def level_of(stream_key, extent, pieces, smallest, top_value):
    def one(position, parts):
        heights = jax.random.uniform(jax.random.fold_in(jax.random.fold_in(stream_key, 6), position), (parts,), jnp.float32, smallest / len(pieces), top_value / len(pieces))
        return jnp.repeat(jnp.exp(heights), extent[position] // parts).reshape((-1,) + (1,) * (len(extent) - position - 1))

    level = one(*pieces[0])
    for cut in pieces[1:]:
        level = level * one(*cut)
    return level


def bell_draw(own_key, extent, spread, reach, cuts=(), kind=jnp.bfloat16):
    drawn = spread * jax.random.normal(own_key, extent, jnp.float32)
    if cuts:
        drawn = drawn * level_of(own_key, extent, cuts, -0.22, 0.18)
    return jnp.clip(drawn, -reach, reach).astype(kind)


def noise_with(rng, dims, deviation, limit, cuts, heavy, dtype=jnp.bfloat16):
    result = deviation * jax.random.normal(rng, dims, jnp.float32)
    if cuts:
        result = result * level_of(rng, dims, cuts, -0.22, 0.18)
    return jnp.clip(strengthened(result, jax.random.fold_in(rng, 3), *heavy), -limit, limit).astype(dtype)


def setup_inputs(seed: int = 0) -> dict:
    arg_keys = jax.random.split(jax.random.key(seed), 4)
    tensor = noise_with(arg_keys[0], (K, NI, NJ), NI, 12288.0, ((1, 16), (2, 32)), (2, 1, 32, 2.75), jnp.float32)
    factor_b = bell_draw(arg_keys[1], (J_DEV, N_COL * R), 1.0, 6.0, ((0, 16), (1, 32)), jnp.float32)
    factor_c = bell_draw(arg_keys[2], (K, R), 1.0, 6.0, (), jnp.float32)
    return dict(tensor=tensor, factor_b=factor_b, factor_c=factor_c)


highest = lax.Precision.HIGHEST
epsilon = 1e-06

def product(left, right):
    return jnp.dot(left.astype(jnp.float32), right.astype(jnp.float32), precision=highest, preferred_element_type=jnp.float32)

def solve_rows(right_side, system):
    lower_factor = jnp.linalg.cholesky(system)
    halfway = lax.linalg.triangular_solve(lower_factor, right_side, left_side=False, lower=True, transpose_a=True)
    return lax.linalg.triangular_solve(lower_factor, halfway, left_side=False, lower=True, transpose_a=False)

def column_scale(gram_raw, count):
    return jnp.sqrt(jnp.diagonal(gram_raw) / count + epsilon)

def reference(tensor, factor_b, factor_c):
    whole_b = factor_b.reshape(J_DEV, N_COL, R).transpose(1, 0, 2).reshape(NJ, R)
    gram_c = product(factor_c.T, factor_c)
    gram_b = product(whole_b.T, whole_b)
    mttkrp_a = jnp.zeros((NI, R), jnp.float32)
    for member in range(K):
        mttkrp_a = mttkrp_a + product(tensor[member], whole_b) * factor_c[member]
    raw_a = solve_rows(mttkrp_a, gram_b * gram_c)
    gram_raw_a = product(raw_a.T, raw_a)
    scale_a = column_scale(gram_raw_a, NI)
    new_a = raw_a / scale_a
    gram_a = gram_raw_a / (scale_a[:, None] * scale_a[None, :])
    mttkrp_b = jnp.zeros((NJ, R), jnp.float32)
    for member in range(K):
        contracted = lax.dot_general(tensor[member].astype(jnp.float32), new_a.astype(jnp.float32), (((0,), (0,)), ((), ())), precision=highest, preferred_element_type=jnp.float32)
        mttkrp_b = mttkrp_b + contracted * factor_c[member]
    raw_b = solve_rows(mttkrp_b, gram_a * gram_c)
    gram_raw_b = product(raw_b.T, raw_b)
    scale_b = column_scale(gram_raw_b, NJ)
    next_b = raw_b / scale_b
    gram_next_b = gram_raw_b / (scale_b[:, None] * scale_b[None, :])
    slab_rows = []
    for member in range(K):
        slab_rows.append(lax.optimization_barrier(jnp.sum(product(tensor[member], next_b) * new_a, axis=0)))
    mttkrp_c = jnp.stack(slab_rows)
    new_c = solve_rows(mttkrp_c, gram_a * gram_next_b)
    new_b = next_b.reshape(N_COL, J_DEV, R).transpose(1, 0, 2).reshape(J_DEV, N_COL * R)
    return (new_a, new_b, new_c)
```

```python
import functools

import jax
import jax.numpy as jnp
from jax import lax
from jax.experimental import pallas as pl
from jax.experimental.pallas import tpu as pltpu
from jax.sharding import PartitionSpec as P

f32 = jnp.float32
bf16 = jnp.bfloat16
highest = lax.Precision.HIGHEST
epsilon = 1e-06
EXCHANGES = 19


def dot(left, right):
    return jnp.dot(left, right, precision=highest, preferred_element_type=f32)


def lane_of(tile, index):
    return jnp.take_along_axis(tile, jnp.full(tile.shape, index, jnp.int32), axis=1)


def row_of(tile, k):
    return jnp.broadcast_to(tile[k : k + 1], tile.shape)


def added(parts):
    while len(parts) > 1:
        parts = [a + b for a, b in zip(parts[::2], parts[1::2])] + parts[len(parts) & ~1 :]
    return parts[0]


def pivot_panel(tile, p):
    lane = lax.broadcasted_iota(jnp.int32, (8, 128), 1)
    sub = lax.broadcasted_iota(jnp.int32, (8, 128), 0)
    d = [lane_of(tile, p * 8 + k) for k in range(8)]
    for j in range(8):
        here = sub == j
        c = jnp.where(here, -1.0, d[j]) * (1.0 / row_of(d[j], j))
        d = [-c if k == j else jnp.where(here, 0.0, d[k]) - c * row_of(d[k], j) for k in range(8)]
    rows = jnp.where(lane // 8 == p, jnp.where(lane % 8 == sub, 1.0, 0.0), tile)
    return added([d[k] * row_of(rows, k) for k in range(8)])


def cleared(tile, p, pivot):
    lane = lax.broadcasted_iota(jnp.int32, (8, 128), 1)
    return jnp.where(lane // 8 == p, 0.0, tile) - added(
        [lane_of(tile, p * 8 + k) * row_of(pivot, k) for k in range(8)]
    )


def thirds(x):
    high = x.astype(bf16).astype(f32)
    rest = x - high
    middle = rest.astype(bf16).astype(f32)
    return high, middle, rest - middle


def outer(left, right):
    lh, lm, ll = thirds(left)
    rh, rm, rl = thirds(right)
    lhs = jnp.concatenate([lh, lh, lm, lh, ll, lm], axis=0).astype(bf16)
    rhs = jnp.concatenate([rh, rm, rh, rl, rh, rm], axis=0).astype(bf16)
    return lax.dot_general(lhs, rhs, (((0,), (0,)), ((), ())), preferred_element_type=f32)


def invert_half(t):
    n = t.shape[0] // 8
    lane = lax.broadcasted_iota(jnp.int32, (8, 128), 1)
    lanes = lax.broadcasted_iota(jnp.int32, (128, 128), 1)

    def step(p, tile, pivot, last):
        if not last:
            ahead = t[pl.ds(pl.multiple_of((p + 1) * 8, 8), 8), :]
            tile_next = cleared(ahead, p, pivot)
            pivot_next = pivot_panel(tile_next, p + 1)
        update = outer(jnp.where(lane < 8 * p, -tile, tile), pivot)
        t[...] = jnp.where(lanes // 8 == p, 0.0, t[...]) - update
        t[pl.ds(pl.multiple_of(p * 8, 8), 8), :] = pivot
        return None if last else (tile_next, pivot_next)

    first = t[0:8, :]
    held = lax.fori_loop(0, n - 1, lambda p, v: step(p, *v, False), (first, pivot_panel(first, 0)))
    step(n - 1, *held, True)


def invert(system, t, between=None):
    b, bt = system[0:128, 128:256], system[128:256, 0:128]
    t[...] = system[0:128, 0:128]
    invert_half(t)
    if between is not None:
        between()
    a = t[...]
    w, wt = dot(a, b), dot(bt, a)
    t[...] = system[128:256, 128:256] - dot(bt, w)
    invert_half(t)
    d = t[...]
    v, vt = dot(w, d), dot(d, wt)
    return jnp.concatenate(
        [jnp.concatenate([a + dot(v, wt), -v], axis=1), jnp.concatenate([-vt, d], axis=1)], axis=0
    )


def sweep(
    nz, nc, tensor, factor_b, factor_c, new_a, new_b, new_c,
    tensor_t, gram_c, across_b, block_b, flipped, pieces, landed, owned, ringed, chunks, grams,
    out_m, in_m, rows_a, block_a, contracted, out_b, in_b, rows_b, pieces_c, landed_c, summed_c, around_c,
    whole_c, ringed_c, system, half, sent, received,
):
    nq = nc // 2
    members, wide_a, wide_b = tensor.shape
    rank = factor_b.shape[1]
    z, c = lax.axis_index("row"), lax.axis_index("col")
    q, core = c // 2, c % 2

    barrier = pltpu.get_barrier_semaphore()

    def greet(k, carry):
        other = lax.rem(z + k, nz)
        pl.semaphore_signal(barrier, inc=1, device_id=(other, c), device_id_type=pl.DeviceIdType.MESH)
        pl.semaphore_signal(barrier, inc=1, device_id=(other, c + 1 - 2 * core), device_id_type=pl.DeviceIdType.MESH)
        return carry

    def greet_col(k, carry):
        pl.semaphore_signal(barrier, inc=1, device_id=(z, lax.rem(c + k, nc)), device_id_type=pl.DeviceIdType.MESH)
        return carry

    lax.fori_loop(1, nz, greet, 0)
    lax.fori_loop(1, nc, greet_col, 0)

    for m in range(members):
        tensor_t[m] = jnp.transpose(tensor[m])
    by_row = factor_c[...]
    gram_c[...] = lax.dot_general(
        by_row, by_row, (((0,), (0,)), ((), ())), precision=highest, preferred_element_type=f32
    )
    pl.semaphore_wait(barrier, 2 * (nz - 1) + nc - 1)

    def copy(src, dst, which, to):
        pltpu.make_async_remote_copy(
            src_ref=src, dst_ref=dst, send_sem=sent.at[which], recv_sem=received.at[which],
            device_id=to, device_id_type=pl.DeviceIdType.MESH,
        ).start()

    totals = []

    def send_z(which, src, dst, scatter=False):
        def one(k, carry):
            other = lax.rem(z + k, nz)
            copy(src.at[other] if scatter else src, dst.at[z], which, (other, c))
            return carry
        lax.fori_loop(1, nz, one, 0)
        totals.append((which, dst.at[pl.ds(0, nz - 1)]))
        dst[z] = src[z] if scatter else src[...]

    def send_zz(which, src, dst):
        me = 2 * z + core
        def one(k, carry):
            other = lax.rem(me + k, 2 * nz)
            copy(src.at[other // 2], dst.at[me], which, (other // 2, 2 * q + other % 2))
            return carry
        lax.fori_loop(1, 2 * nz, one, 0)
        totals.append((which, dst.at[pl.ds(0, 2 * nz - 1)]))
        dst[me] = src[z]

    def send_q(which, src, dst):
        def one(k, carry):
            other = lax.rem(q + k, nq)
            copy(src, dst.at[q], which, (z, 2 * other + core))
            return carry
        lax.fori_loop(1, nq, one, 0)
        totals.append((which, dst.at[pl.ds(0, nq - 1)]))
        dst[q] = src[...]

    def send_c(which, src, dst, scatter=False):
        def one(k, carry):
            other = lax.rem(c + k, nc)
            copy(src.at[other // 2] if scatter else src, dst.at[c], which, (z, other))
            return carry
        lax.fori_loop(1, nc, one, 0)
        totals.append((which, dst.at[pl.ds(0, nc - 1)]))
        dst[c] = src[q] if scatter else src[...]

    def arrived(which):
        whole = dict(totals)[which]
        pltpu.make_async_remote_copy(
            src_ref=whole, dst_ref=whole, send_sem=sent.at[which], recv_sem=received.at[which],
            device_id=(z, c), device_id_type=pl.DeviceIdType.MESH,
        ).wait_recv()

    def left(which):
        whole = dict(totals)[which]
        pltpu.make_async_remote_copy(
            src_ref=whole, dst_ref=whole, send_sem=sent.at[which], recv_sem=received.at[which],
            device_id=(z, c), device_id_type=pl.DeviceIdType.MESH,
        ).wait_send()

    def sum_of(ref):
        total = ref[0]
        for k in range(1, ref.shape[0]):
            total = total + ref[k]
        return total

    share = rank // nq
    part = share // nz

    def gram_start(turn, block, both):
        depth = block.shape[0]
        flipped[:, 0:depth] = jnp.transpose(block)
        chunk = dot(flipped[pl.ds(pl.multiple_of(q * share, 8), share), 0:depth], block)
        for k in range(nz):
            pieces[turn, k] = chunk[k * part : (k + 1) * part]
        if both:
            send_zz(3 * turn, pieces.at[turn], landed.at[turn])
        else:
            send_z(3 * turn, pieces.at[turn], landed.at[turn, pl.ds(0, nz)], True)

    def gram_middle(turn, both):
        arrived(3 * turn)
        owned[turn] = sum_of(landed.at[turn] if both else landed.at[turn, pl.ds(0, nz)])
        send_z(3 * turn + 1, owned.at[turn], ringed.at[turn])

    def gram_last(turn):
        arrived(3 * turn + 1)
        for k in range(nz):
            chunks[turn, k * part : (k + 1) * part, :] = ringed[turn, k]
        send_q(3 * turn + 2, chunks.at[turn], grams.at[turn])

    def gram_of(turn):
        arrived(3 * turn + 2)
        return grams[turn].reshape(rank, rank)

    def scales(gram, count):
        one = lax.broadcasted_iota(jnp.int32, gram.shape, 0) == lax.broadcasted_iota(jnp.int32, gram.shape, 1)
        diagonal = jnp.where(one, gram, 0.0)
        return (
            jnp.sqrt(jnp.sum(diagonal, axis=0, keepdims=True) / count + epsilon),
            jnp.sqrt(jnp.sum(diagonal, axis=1, keepdims=True) / count + epsilon),
        )

    send_q(9, factor_b, across_b.at[0])
    send_z(10, factor_b, block_b.at[0])
    arrived(9)
    gram_start(0, across_b[0].reshape(-1, rank), True)
    gram_middle(0, True)
    gram_last(0)
    arrived(10)
    products = dot(tensor[...].reshape(members * wide_a, wide_b), block_b[0].reshape(-1, rank))
    products = products.reshape(members, wide_a, rank)
    sums = products[0] * by_row[0:1]
    for m in range(1, members):
        sums = sums + products[m] * by_row[m : m + 1]
    out_m[...] = sums.reshape(nq, 8, rank)
    send_c(11, out_m, in_m, True)
    system[...] = gram_of(0) * gram_c[...]
    inverse = invert(system, half)
    arrived(11)
    rows_a[...] = dot(sum_of(in_m), inverse)

    send_q(12, rows_a, block_a)
    arrived(12)
    whole_a = block_a[...].reshape(wide_a, rank)
    gram_start(1, whole_a, False)
    contracted[...] = dot(
        tensor_t[...].reshape(members * wide_b, wide_a), whole_a
    ).reshape(members, wide_b, rank)
    gram_middle(1, False)
    sums = contracted[0] * by_row[0:1]
    for m in range(1, members):
        sums = sums + contracted[m] * by_row[m : m + 1]
    out_b[...] = sums.reshape(nz, -1, rank)
    gram_last(1)
    send_z(13, out_b, in_b, True)
    gram = gram_of(1)
    scale_a, scale_a_down = scales(gram, wide_a * nz)
    gram_a = gram / (scale_a * scale_a_down)
    system[...] = gram_a * gram_c[...]
    gram_c[...] = gram_a
    mine = rows_a[...] / scale_a
    new_a[...] = jnp.where(core == 0, mine[0:4], mine[4:8])
    inverse = invert(system, half)
    arrived(13)
    rows_b[...] = dot(sum_of(in_b) / scale_a, inverse)

    send_q(14, rows_b, across_b.at[1])
    send_z(15, rows_b, block_b.at[1])
    arrived(14)
    gram_start(2, across_b[1].reshape(-1, rank), True)
    gram_middle(2, True)
    gram_last(2)
    gram = gram_of(2)
    scale_b, scale_b_down = scales(gram, wide_b * nc)
    system[...] = gram_c[...] * (gram / (scale_b * scale_b_down))
    new_b[...] = rows_b[...] / scale_b
    arrived(15)
    next_b = block_b[1].reshape(-1, rank) / scale_b
    step = 16 // nz
    for m in range(members):
        row = jnp.sum(contracted[m] * next_b, axis=0, keepdims=True) / scale_a
        for side in range(2):
            at = 2 * m + side
            pieces_c[at // step, at % step : at % step + 1, :] = row[:, 128 * side : 128 * side + 128]
    send_z(16, pieces_c, landed_c, True)

    def between():
        arrived(16)
        summed_c[...] = sum_of(landed_c)
        send_c(17, summed_c, around_c)

    inverse = invert(system, half, between)
    arrived(17)
    whole_c[...] = sum_of(around_c)
    send_z(18, whole_c, ringed_c)
    arrived(18)
    halves = [ringed_c[at // step, at % step : at % step + 1, :] for at in range(16)]
    right_side = jnp.concatenate(
        [jnp.concatenate(halves[0::2], axis=0), jnp.concatenate(halves[1::2], axis=0)], axis=1
    )
    new_c[...] = dot(right_side, inverse)
    for which, _ in totals:
        left(which)


def solution(mesh):
    nz, nc = mesh.shape["row"], mesh.shape["col"]
    nq = nc // 2

    def on_device(tensor, factor_b, factor_c):
        members, wide_a, wide_b = tensor.shape
        deep_b, rank = factor_b.shape
        share = rank // nq
        part = share // nz
        step = 16 // nz
        memory = [
            (members, wide_b, wide_a),
            (rank, rank),
            (2, nq, deep_b, rank),
            (2, nz, deep_b, rank),
            (rank, max(nq * deep_b, wide_a)),
            (3, nz, part, rank),
            (3, 2 * nz, part, rank),
            (3, part, rank),
            (3, nz, part, rank),
            (3, share, rank),
            (3, nq, share, rank),
            (nq, 8, rank),
            (nc, 8, rank),
            (8, rank),
            (nq, 8, rank),
            (members, wide_b, rank),
            (nz, deep_b, rank),
            (nz, deep_b, rank),
            (deep_b, rank),
            (nz, step, 128),
            (nz, step, 128),
            (step, 128),
            (nc, step, 128),
            (step, 128),
            (nz, step, 128),
            (rank, rank),
            (128, 128),
        ]
        return pl.pallas_call(
            functools.partial(sweep, nz, nc),
            out_shape=(
                jax.ShapeDtypeStruct((wide_a // nc, rank), f32),
                jax.ShapeDtypeStruct((deep_b, rank), f32),
                jax.ShapeDtypeStruct((members, rank), f32),
            ),
            in_specs=[pl.BlockSpec(memory_space=pltpu.VMEM)] * 3,
            out_specs=tuple([pl.BlockSpec(memory_space=pltpu.VMEM)] * 3),
            scratch_shapes=[pltpu.VMEM(shape, f32) for shape in memory]
            + [pltpu.SemaphoreType.DMA((EXCHANGES,)), pltpu.SemaphoreType.DMA((EXCHANGES,))],
            compiler_params=pltpu.CompilerParams(
                collective_id=0, has_side_effects=True, vmem_limit_bytes=40 * 1024 * 1024
            ),
        )(tensor, factor_b, factor_c)

    return jax.shard_map(
        on_device,
        mesh=mesh,
        in_specs=(P(None, "row", "col"), P("row", "col"), P()),
        out_specs=(P(("row", "col"), None), P("row", "col"), P()),
        check_vma=False,
    )
```

```python
import functools

import jax
import jax.numpy as jnp
from jax import lax
from jax.experimental import pallas as pl
from jax.experimental.pallas import tpu as pltpu
from jax.sharding import PartitionSpec as P

f32 = jnp.float32
bf16 = jnp.bfloat16
highest = lax.Precision.HIGHEST
epsilon = 1e-06
EXCHANGES = 20
MESH = pl.DeviceIdType.MESH


def dot(left, right):
    return jnp.dot(left, right, precision=highest, preferred_element_type=f32)


def lane_of(tile, index):
    return jnp.take_along_axis(tile, jnp.full(tile.shape, index, jnp.int32), axis=1)


def row_of(tile, k):
    return jnp.broadcast_to(tile[k : k + 1], tile.shape)


def added(parts):
    while len(parts) > 1:
        parts = [a + b for a, b in zip(parts[::2], parts[1::2])] + parts[len(parts) & ~1 :]
    return parts[0]


def pivot_panel(tile, p):
    lane = lax.broadcasted_iota(jnp.int32, (8, 128), 1)
    sub = lax.broadcasted_iota(jnp.int32, (8, 128), 0)
    d = [lane_of(tile, p * 8 + k) for k in range(8)]
    for j in range(8):
        here = sub == j
        c = jnp.where(here, -1.0, d[j]) * (1.0 / row_of(d[j], j))
        d = [-c if k == j else jnp.where(here, 0.0, d[k]) - c * row_of(d[k], j) for k in range(8)]
    rows = jnp.where(lane // 8 == p, jnp.where(lane % 8 == sub, 1.0, 0.0), tile)
    return added([d[k] * row_of(rows, k) for k in range(8)])


def cleared(tile, p, pivot):
    lane = lax.broadcasted_iota(jnp.int32, (8, 128), 1)
    return jnp.where(lane // 8 == p, 0.0, tile) - added(
        [lane_of(tile, p * 8 + k) * row_of(pivot, k) for k in range(8)]
    )


def thirds(x):
    high = x.astype(bf16).astype(f32)
    rest = x - high
    middle = rest.astype(bf16).astype(f32)
    return high, middle, rest - middle


def outer(left, right):
    lh, lm, ll = thirds(left)
    rh, rm, rl = thirds(right)
    lhs = jnp.concatenate([lh, lh, lm, lh, ll, lm], axis=0).astype(bf16)
    rhs = jnp.concatenate([rh, rm, rh, rl, rh, rm], axis=0).astype(bf16)
    return lax.dot_general(lhs, rhs, (((0,), (0,)), ((), ())), preferred_element_type=f32)


def invert_half(t):
    n = t.shape[0] // 8
    lane = lax.broadcasted_iota(jnp.int32, (8, 128), 1)
    lanes = lax.broadcasted_iota(jnp.int32, (128, 128), 1)

    def step(p, tile, pivot, last):
        if not last:
            ahead = t[pl.ds(pl.multiple_of((p + 1) * 8, 8), 8), :]
            tile_next = cleared(ahead, p, pivot)
            pivot_next = pivot_panel(tile_next, p + 1)
        update = outer(jnp.where(lane < 8 * p, -tile, tile), pivot)
        t[...] = jnp.where(lanes // 8 == p, 0.0, t[...]) - update
        t[pl.ds(pl.multiple_of(p * 8, 8), 8), :] = pivot
        return None if last else (tile_next, pivot_next)

    first = t[0:8, :]
    held = lax.fori_loop(0, n - 1, lambda p, v: step(p, *v, False), (first, pivot_panel(first, 0)))
    step(n - 1, *held, True)


def invert(system, t, between=None):
    b, bt = system[0:128, 128:256], system[128:256, 0:128]
    t[...] = system[0:128, 0:128]
    invert_half(t)
    if between is not None:
        between()
    a = t[...]
    w, wt = dot(a, b), dot(bt, a)
    t[...] = system[128:256, 128:256] - dot(bt, w)
    invert_half(t)
    d = t[...]
    v, vt = dot(w, d), dot(d, wt)
    return jnp.concatenate(
        [jnp.concatenate([a + dot(v, wt), -v], axis=1), jnp.concatenate([-vt, d], axis=1)], axis=0
    )


def dot_first(left, right):
    return lax.dot_general(
        left, right, (((0,), (0,)), ((), ())), precision=highest, preferred_element_type=f32
    )


def sweep(
    nz, nc, tensor_in, factor_b_in, factor_c_in, new_a, new_b, new_c,
    tensor, factor_b, factor_c, tensor_t, gram_c, block_b, partial, landed, owned, grams,
    out_m, in_m, rows_m, ring_m, block_m, contracted, out_b, near_b, part_b, far_b, rows_b,
    out_c, in_c, half_c, ring_c, side_c, system, half, sent, received, loaded,
):
    nq, nk = nc // 2, nz // 4
    z, c = lax.axis_index("row"), lax.axis_index("col")
    q, core = c // 2, c % 2
    class_z, place_z = z % 4, z // 4

    loads = [
        pltpu.make_async_copy(src, dst, loaded.at[i])
        for i, (src, dst) in enumerate(((factor_b_in, factor_b), (tensor_in, tensor), (factor_c_in, factor_c)))
    ]
    for load in loads:
        load.start()

    barrier = pltpu.get_barrier_semaphore()

    def greet_z(k, carry):
        pl.semaphore_signal(barrier, inc=1, device_id=(lax.rem(z + k, nz), c), device_id_type=MESH)
        return carry

    def greet_c(k, carry):
        pl.semaphore_signal(barrier, inc=1, device_id=(z, lax.rem(c + k, nc)), device_id_type=MESH)
        return carry

    lax.fori_loop(1, nz, greet_z, 0)
    lax.fori_loop(1, nc, greet_c, 0)

    for load in loads:
        load.wait()
    members, wide_a, wide_b = tensor.shape
    rank = factor_b.shape[1]
    for m in range(members):
        tensor_t[m] = jnp.transpose(tensor[m])
    by_row = factor_c[...]
    gram_c[...] = dot_first(by_row, by_row)
    pl.semaphore_wait(barrier, nz - 1 + nc - 1)

    def copy(which, src, dst, to):
        return pltpu.make_async_remote_copy(
            src_ref=src, dst_ref=dst, send_sem=sent.at[which], recv_sem=received.at[which],
            device_id=to, device_id_type=MESH,
        )

    totals = {}

    def over(which, whole):
        totals[which] = whole

    def arrived(which):
        if which in totals:
            copy(which, totals[which], totals[which], (z, c)).wait_recv()

    def send_all_z(which, src, dst):
        def one(k, carry):
            copy(which, src, dst.at[z], (lax.rem(z + k, nz), c)).start()
            return carry
        lax.fori_loop(1, nz, one, 0)
        over(which, dst.at[pl.ds(0, nz - 1)])
        dst[z] = src[...]

    def send_q(which, src, dst, scatter=False):
        def one(k, carry):
            other = lax.rem(q + k, nq)
            copy(which, src.at[2 * other + core] if scatter else src, dst.at[q], (z, 2 * other + core)).start()
            return carry
        lax.fori_loop(1, nq, one, 0)
        if nq > 1:
            over(which, dst.at[pl.ds(0, nq - 1)])
        dst[q] = src[c] if scatter else src[...]

    def send_c(which, src, dst, pick=None):
        def one(k, carry):
            other = lax.rem(c + k, nc)
            copy(which, src.at[pick(other)] if pick else src, dst.at[c], (z, other)).start()
            return carry
        lax.fori_loop(1, nc, one, 0)
        over(which, dst.at[pl.ds(0, nc - 1)])
        dst[c] = src[pick(c)] if pick else src[...]

    def sum_of(ref):
        total = ref[0]
        for k in range(1, ref.shape[0]):
            total = total + ref[k]
        return total

    def gather_far(which, src, dst):
        for k in range(1, nk):
            copy(which, src, dst.at[class_z, place_z], (lax.rem(z + 4 * k, nz), c)).start()
        if nk > 1:
            over(which, dst.at[0, pl.ds(0, nk - 1)])
        dst[class_z, place_z] = src[...]

    def gather_near(which, dst):
        for k in (1, nz - 1, 2):
            copy(which, dst.at[class_z], dst.at[class_z], (lax.rem(z + k, nz), c)).start()
        over(which, dst.at[pl.ds(0, 3)])

    def gathered(ref):
        return jnp.concatenate([ref[k % 4, k // 4] for k in range(nz)], axis=0)

    def scatter_near(which, src, dst):
        for slot, k in enumerate((1, nz - 1, 2)):
            copy(which, src.at[lax.rem(z + k, 4)], dst.at[slot], (lax.rem(z + k, nz), c)).start()
        over(which, dst.at[pl.ds(0, 3)])

    def scatter_far(which, src, dst):
        for k in range(1, nk):
            other = lax.rem(z + 4 * k, nz)
            copy(which, src.at[other // 4], dst.at[k - 1], (other, c)).start()
        if nk > 1:
            over(which, dst.at[pl.ds(0, nk - 1)])

    part = rank // nc

    def gram_start(turn, block, both):
        partial[turn] = dot_first(block, block).reshape(nc, part, rank)
        if both:
            send_c(3 * turn, partial.at[turn], landed.at[turn], lambda other: other)
        else:
            send_q(3 * turn, partial.at[turn], landed.at[turn, pl.ds(0, nq)], True)

    def gram_middle(turn, both):
        arrived(3 * turn)
        owned[turn] = sum_of(landed.at[turn] if both else landed.at[turn, pl.ds(0, nq)])
        send_c(3 * turn + 1, owned.at[turn], grams.at[turn])

    def gram_of(turn):
        arrived(3 * turn + 1)
        return grams[turn].reshape(rank, rank)

    def scales(gram, count):
        one = lax.broadcasted_iota(jnp.int32, gram.shape, 0) == lax.broadcasted_iota(jnp.int32, gram.shape, 1)
        diagonal = jnp.where(one, gram, 0.0)
        return (
            jnp.sqrt(jnp.sum(diagonal, axis=0, keepdims=True) / count + epsilon),
            jnp.sqrt(jnp.sum(diagonal, axis=1, keepdims=True) / count + epsilon),
        )

    gather_far(2, factor_b, block_b.at[0])
    arrived(2)
    gather_near(5, block_b.at[0])
    arrived(5)
    whole_b = gathered(block_b.at[0])
    gram_start(0, whole_b, True)
    products = dot(tensor[...].reshape(members * wide_a, wide_b), whole_b).reshape(members, wide_a, rank)
    sums = products[0] * by_row[0:1]
    for m in range(1, members):
        sums = sums + products[m] * by_row[m : m + 1]
    out_m[...] = sums.reshape(nq, 8, rank)
    send_c(9, out_m, in_m, lambda other: other // 2)
    gram_middle(0, True)
    arrived(9)
    rows_m[...] = sum_of(in_m)
    send_all_z(10, rows_m, ring_m)
    send_q(11, rows_m, block_m)
    system[...] = gram_of(0) * gram_c[...]
    inverse = invert(system, half)

    arrived(10)
    gram_start(1, dot(ring_m[...].reshape(nz * 8, rank), inverse), False)
    arrived(11)
    whole_a = dot(block_m[...].reshape(wide_a, rank), inverse)
    contracted[...] = dot(
        tensor_t[...].reshape(members * wide_b, wide_a), whole_a
    ).reshape(members, wide_b, rank)
    sums = contracted[0] * by_row[0:1]
    for m in range(1, members):
        sums = sums + contracted[m] * by_row[m : m + 1]
    sums = sums.reshape(nz, -1, rank)
    for k in range(nz):
        out_b[k % 4, k // 4] = sums[k]
    scatter_near(12, out_b, near_b)
    gram_middle(1, False)
    raw_a = dot(rows_m[...], inverse)
    arrived(12)
    part_b[...] = (out_b[class_z] + near_b[0]) + (near_b[1] + near_b[2])
    scatter_far(13, part_b, far_b)
    gram = gram_of(1)
    scale_a, scale_a_down = scales(gram, wide_a * nz)
    gram_a = gram / (scale_a * scale_a_down)
    system[...] = gram_a * gram_c[...]
    gram_c[...] = gram_a

    def rows_b_known():
        raw_a_scaled = raw_a / scale_a
        new_a[...] = jnp.where(core == 0, raw_a_scaled[0:4], raw_a_scaled[4:8])
        arrived(13)
        total = part_b[place_z]
        for k in range(nk - 1):
            total = total + far_b[k]
        rows_b[...] = total / scale_a
        gather_far(14, rows_b, block_b.at[1])

    inverse = invert(system, half, rows_b_known)
    arrived(14)
    gather_near(15, block_b.at[1])
    for m in range(members):
        contracted[m] = contracted[m] / scale_a
    arrived(15)

    raw_b = dot(gathered(block_b.at[1]), inverse)
    gram_start(2, raw_b, True)
    sums = jnp.concatenate(
        [jnp.sum(contracted[m] * raw_b, axis=0, keepdims=True) for m in range(members)], axis=0
    )
    out_c[0] = sums[:, 0:128]
    out_c[1] = sums[:, 128:256]
    send_c(16, out_c, in_c, lambda other: other % 2)
    raw_b_own = dot(rows_b[...], inverse)
    gram_middle(2, True)
    arrived(16)
    half_c[...] = sum_of(in_c)
    send_all_z(17, half_c, ring_c)
    gram = gram_of(2)
    scale_b, scale_b_down = scales(gram, wide_b * nc)
    system[...] = gram_c[...] * (gram / (scale_b * scale_b_down))
    new_b[...] = raw_b_own / scale_b

    def half_known():
        arrived(17)
        side_c[core] = sum_of(ring_c)
        copy(18, side_c.at[core], side_c.at[core], (z, c + 1 - 2 * core)).start()
        over(18, side_c.at[0])

    inverse = invert(system, half, half_known)
    arrived(18)
    new_c[...] = dot(jnp.concatenate([side_c[0], side_c[1]], axis=1) / scale_b, inverse)
    for which, whole in totals.items():
        copy(which, whole, whole, (z, c)).wait_send()


def solution(mesh):
    nz, nc = mesh.shape["row"], mesh.shape["col"]
    nq, nk = nc // 2, nz // 4

    def on_device(tensor, factor_b, factor_c):
        members, wide_a, wide_b = tensor.shape
        deep_b, rank = factor_b.shape
        part = rank // nc
        memory = [
            tensor.shape,
            factor_b.shape,
            factor_c.shape,
            (members, wide_b, wide_a),
            (rank, rank),
            (2, 4, nk, deep_b, rank),
            (3, nc, part, rank),
            (3, nc, part, rank),
            (3, part, rank),
            (3, nc, part, rank),
            (nq, 8, rank),
            (nc, 8, rank),
            (8, rank),
            (nz, 8, rank),
            (nq, 8, rank),
            (members, wide_b, rank),
            (4, nk, deep_b, rank),
            (3, nk, deep_b, rank),
            (nk, deep_b, rank),
            (max(nk - 1, 1), deep_b, rank),
            (deep_b, rank),
            (2, members, 128),
            (nc, members, 128),
            (members, 128),
            (nz, members, 128),
            (2, members, 128),
            (rank, rank),
            (128, 128),
        ]
        return pl.pallas_call(
            functools.partial(sweep, nz, nc),
            out_shape=(
                jax.ShapeDtypeStruct((wide_a // nc, rank), f32),
                jax.ShapeDtypeStruct((deep_b, rank), f32),
                jax.ShapeDtypeStruct((members, rank), f32),
            ),
            in_specs=[pl.BlockSpec(memory_space=pl.ANY)] * 3,
            out_specs=tuple([pl.BlockSpec(memory_space=pltpu.VMEM)] * 3),
            scratch_shapes=[pltpu.VMEM(shape, f32) for shape in memory]
            + [pltpu.SemaphoreType.DMA((EXCHANGES,)), pltpu.SemaphoreType.DMA((EXCHANGES,))]
            + [pltpu.SemaphoreType.DMA((3,))],
            compiler_params=pltpu.CompilerParams(
                collective_id=0, has_side_effects=True, vmem_limit_bytes=40 * 1024 * 1024
            ),
        )(tensor, factor_b, factor_c)

    return jax.shard_map(
        on_device,
        mesh=mesh,
        in_specs=(P(None, "row", "col"), P("row", "col"), P()),
        out_specs=(P(("row", "col"), None), P("row", "col"), P()),
        check_vma=False,
    )
```

```python
import functools

import jax
import jax.numpy as jnp
from jax import lax
from jax.experimental import pallas as pl
from jax.experimental.pallas import tpu as pltpu
from jax.sharding import PartitionSpec as P

f32 = jnp.float32
bf16 = jnp.bfloat16
highest = lax.Precision.HIGHEST
epsilon = 1e-06
EXCHANGES = 32
MESH = pl.DeviceIdType.MESH


def dot(left, right):
    return jnp.dot(left, right, precision=highest, preferred_element_type=f32)


def lane_of(tile, index):
    return jnp.take_along_axis(tile, jnp.full(tile.shape, index, jnp.int32), axis=1)


def row_of(tile, k):
    return jnp.broadcast_to(tile[k : k + 1], tile.shape)


def added(parts):
    while len(parts) > 1:
        parts = [a + b for a, b in zip(parts[::2], parts[1::2])] + parts[len(parts) & ~1 :]
    return parts[0]


def pivot_panel(tile, p):
    lane = lax.broadcasted_iota(jnp.int32, (8, 128), 1)
    sub = lax.broadcasted_iota(jnp.int32, (8, 128), 0)
    d = [lane_of(tile, p * 8 + k) for k in range(8)]
    for j in range(8):
        here = sub == j
        c = jnp.where(here, -1.0, d[j])
        products = [None if k == j else c * row_of(d[k], j) for k in range(8)]
        r = 1.0 / row_of(d[j], j)
        d = [-c * r if k == j else jnp.where(here, 0.0, d[k]) - products[k] * r for k in range(8)]
    rows = jnp.where(lane // 8 == p, jnp.where(lane % 8 == sub, 1.0, 0.0), tile)
    return added([d[k] * row_of(rows, k) for k in range(8)])


def cleared(tile, p, pivot):
    lane = lax.broadcasted_iota(jnp.int32, (8, 128), 1)
    return jnp.where(lane // 8 == p, 0.0, tile) - added(
        [lane_of(tile, p * 8 + k) * row_of(pivot, k) for k in range(8)]
    )


def thirds(x):
    high = x.astype(bf16).astype(f32)
    rest = x - high
    middle = rest.astype(bf16).astype(f32)
    return high, middle, rest - middle


def outer(left, right):
    lh, lm, ll = thirds(left)
    rh, rm, rl = thirds(right)
    lhs = jnp.concatenate([lh, lh, lm, lh, ll, lm], axis=0).astype(bf16)
    rhs = jnp.concatenate([rh, rm, rh, rl, rh, rm], axis=0).astype(bf16)
    return lax.dot_general(lhs, rhs, (((0,), (0,)), ((), ())), preferred_element_type=f32)


def invert_half(t):
    n = t.shape[0] // 8
    lane = lax.broadcasted_iota(jnp.int32, (8, 128), 1)
    lanes = lax.broadcasted_iota(jnp.int32, (128, 128), 1)

    def step(p, tile, pivot, last):
        if not last:
            ahead = t[pl.ds(pl.multiple_of((p + 1) * 8, 8), 8), :]
            tile_next = cleared(ahead, p, pivot)
            pivot_next = pivot_panel(tile_next, p + 1)
        update = outer(jnp.where(lane < 8 * p, -tile, tile), pivot)
        t[...] = jnp.where(lanes // 8 == p, 0.0, t[...]) - update
        t[pl.ds(pl.multiple_of(p * 8, 8), 8), :] = pivot
        return None if last else (tile_next, pivot_next)

    first = t[0:8, :]
    held = lax.fori_loop(
        0, n - 1, lambda p, v: step(p, *v, False), (first, pivot_panel(first, 0)), unroll=3
    )
    step(n - 1, *held, True)


def invert(system, t, between=None):
    b, bt = system[0:128, 128:256], system[128:256, 0:128]
    t[...] = system[0:128, 0:128]
    invert_half(t)
    if between is not None:
        between()
    a = t[...]
    w, wt = dot(a, b), dot(bt, a)
    t[...] = system[128:256, 128:256] - dot(bt, w)
    invert_half(t)
    d = t[...]
    v, vt = dot(w, d), dot(d, wt)
    return jnp.concatenate(
        [jnp.concatenate([a + dot(v, wt), -v], axis=1), jnp.concatenate([-vt, d], axis=1)], axis=0
    )


def dot_first(left, right):
    return lax.dot_general(
        left, right, (((0,), (0,)), ((), ())), precision=highest, preferred_element_type=f32
    )


def sweep(
    nz, nc, tensor_in, factor_b_in, factor_c_in, new_a, new_b, new_c,
    tensor, factor_b, factor_c, tensor_t, gram_c, block_b, partial, landed, owned, grams,
    out_m, in_m, rows_m, ring_m, block_m, contracted, out_b, near_b, part_b, far_b, rows_b,
    out_c, in_c, half_c, ring_c, side_c, system, half, sent, received, loaded,
):
    nq, nk = nc // 2, nz // 4
    z, c = lax.axis_index("row"), lax.axis_index("col")
    q, core = c // 2, c % 2
    class_z, place_z = z % 4, z // 4

    loads = [
        pltpu.make_async_copy(src, dst, loaded.at[i])
        for i, (src, dst) in enumerate(((factor_b_in, factor_b), (tensor_in, tensor), (factor_c_in, factor_c)))
    ]
    for load in loads:
        load.start()

    barrier = pltpu.get_barrier_semaphore()

    def greet_z(k, carry):
        pl.semaphore_signal(barrier, inc=1, device_id=(lax.rem(z + k, nz), c), device_id_type=MESH)
        return carry

    def greet_c(k, carry):
        pl.semaphore_signal(barrier, inc=1, device_id=(z, lax.rem(c + k, nc)), device_id_type=MESH)
        return carry

    lax.fori_loop(1, nz, greet_z, 0)
    lax.fori_loop(1, nc, greet_c, 0)

    for load in loads:
        load.wait()
    members, wide_a, wide_b = tensor.shape
    rank = factor_b.shape[1]
    for m in range(members):
        tensor_t[:, m * wide_a : (m + 1) * wide_a] = jnp.transpose(tensor[m])
    by_row = factor_c[...]
    gram_c[...] = dot_first(by_row, by_row)
    pl.semaphore_wait(barrier, nz - 1 + nc - 1)

    def copy(which, src, dst, to):
        return pltpu.make_async_remote_copy(
            src_ref=src, dst_ref=dst, send_sem=sent.at[which], recv_sem=received.at[which],
            device_id=to, device_id_type=MESH,
        )

    totals = {}

    def hops(k):
        return -(min(k % 4, 4 - k % 4) + min(k // 4, 4 - k // 4))

    def over(which, whole):
        totals[which] = whole

    def arrived(which):
        if which in totals:
            copy(which, totals[which], totals[which], (z, c)).wait_recv()

    def send_all_z(which, src, dst):
        for k in sorted(range(1, nz), key=lambda k: -min(k, nz - k)):
            copy(which, src, dst.at[z], (lax.rem(z + k, nz), c)).start()
        over(which, dst.at[pl.ds(0, nz - 1)])
        dst[z] = src[...]

    def send_q(which, src, dst, scatter=False):
        for k in sorted(range(1, nq), key=hops):
            other = lax.rem(q + k, nq)
            copy(which, src.at[2 * other + core] if scatter else src, dst.at[q], (z, 2 * other + core)).start()
        if nq > 1:
            over(which, dst.at[pl.ds(0, nq - 1)])
        dst[q] = src[c] if scatter else src[...]

    def send_c(which, src, dst, pick=None):
        for k in sorted(range(1, nc), key=lambda k: hops(k // 2)):
            other = lax.rem(c + k, nc)
            copy(which, src.at[pick(other)] if pick else src, dst.at[c], (z, other)).start()
        over(which, dst.at[pl.ds(0, nc - 1)])
        dst[c] = src[pick(c)] if pick else src[...]

    def sum_of(ref):
        total = ref[0]
        for k in range(1, ref.shape[0]):
            total = total + ref[k]
        return total

    far = sorted(range(1, nk), key=lambda k: -min(k, nk - k))

    def to_near(which, block):
        for k in (2, 1, nz - 1):
            copy(which, block, block, (lax.rem(z + k, nz), c)).start()

    def gather_start(which, src, dst):
        for k in far:
            copy(which + k, src, dst.at[class_z, place_z], (lax.rem(z + 4 * k, nz), c)).start()
            over(which + k, dst.at[0, 0])
        dst[class_z, place_z] = src[...]
        to_near(which, dst.at[class_z, place_z])
        over(which, dst.at[pl.ds(0, 3), 0])

    def gather_on(which, dst):
        for k in reversed(far):
            arrived(which + k)
            to_near(which + nk - 1 + k, dst.at[class_z, lax.rem(place_z + nk - k, nk)])
            over(which + nk - 1 + k, dst.at[pl.ds(0, 3), 0])

    def gather_end(which):
        arrived(which)
        for k in reversed(far):
            arrived(which + nk - 1 + k)

    def gathered(ref):
        return jnp.concatenate([ref[k % 4, k // 4] for k in range(nz)], axis=0)

    def scatter_near(which, src, dst):
        for slot, k in enumerate((1, nz - 1, 2)):
            copy(which, src.at[lax.rem(z + k, 4)], dst.at[slot], (lax.rem(z + k, nz), c)).start()
        over(which, dst.at[pl.ds(0, 3)])

    def scatter_far(which, src, dst):
        for k in range(1, nk):
            other = lax.rem(z + 4 * k, nz)
            copy(which, src.at[other // 4], dst.at[k - 1], (other, c)).start()
        if nk > 1:
            over(which, dst.at[pl.ds(0, nk - 1)])

    part = rank // nc

    def gram_start(turn, block, both):
        partial[turn] = dot_first(block, block).reshape(nc, part, rank)
        if both:
            send_c(3 * turn, partial.at[turn], landed.at[turn], lambda other: other)
        else:
            send_q(3 * turn, partial.at[turn], landed.at[turn, pl.ds(0, nq)], True)

    def gram_middle(turn, both):
        arrived(3 * turn)
        owned[turn] = sum_of(landed.at[turn] if both else landed.at[turn, pl.ds(0, nq)])
        send_c(3 * turn + 1, owned.at[turn], grams.at[turn])

    def gram_of(turn):
        arrived(3 * turn + 1)
        return grams[turn].reshape(rank, rank)

    def scales(gram, count):
        one = lax.broadcasted_iota(jnp.int32, gram.shape, 0) == lax.broadcasted_iota(jnp.int32, gram.shape, 1)
        diagonal = jnp.where(one, gram, 0.0)
        return (
            jnp.sqrt(jnp.sum(diagonal, axis=0, keepdims=True) / count + epsilon),
            jnp.sqrt(jnp.sum(diagonal, axis=1, keepdims=True) / count + epsilon),
        )

    gather_start(18, factor_b, block_b.at[0])
    gather_on(18, block_b.at[0])
    gather_end(18)
    whole_b = gathered(block_b.at[0])
    gram_start(0, whole_b, True)
    products = dot(tensor[...].reshape(members * wide_a, wide_b), whole_b).reshape(members, wide_a, rank)
    sums = products[0] * by_row[0:1]
    for m in range(1, members):
        sums = sums + products[m] * by_row[m : m + 1]
    out_m[...] = sums.reshape(nq, 8, rank)
    send_c(9, out_m, in_m, lambda other: other // 2)
    gram_middle(0, True)
    arrived(9)
    rows_m[...] = sum_of(in_m)
    send_all_z(10, rows_m, ring_m)
    send_q(11, rows_m, block_m)
    system[...] = gram_of(0) * gram_c[...]
    inverse = invert(system, half)

    arrived(11)
    whole_a = dot(block_m[...].reshape(wide_a, rank), inverse)
    weighted = jnp.concatenate([whole_a * by_row[m : m + 1] for m in range(members)], axis=0)
    sums = dot(tensor_t[...], weighted).reshape(nz, -1, rank)
    for k in range(nz):
        out_b[k % 4, k // 4] = sums[k]
    scatter_near(12, out_b, near_b)
    arrived(10)
    gram_start(1, dot(ring_m[...].reshape(nz * 8, rank), inverse), False)
    for m in range(members):
        contracted[m] = dot(tensor_t[:, m * wide_a : (m + 1) * wide_a], whole_a)
    raw_a = dot(rows_m[...], inverse)
    arrived(12)
    part_b[...] = (out_b[class_z] + near_b[0]) + (near_b[1] + near_b[2])
    scatter_far(13, part_b, far_b)
    gram_middle(1, False)
    gram = gram_of(1)
    scale_a, scale_a_down = scales(gram, wide_a * nz)
    gram_a = gram / (scale_a * scale_a_down)
    system[...] = gram_a * gram_c[...]
    gram_c[...] = gram_a
    arrived(13)
    total = part_b[place_z]
    for k in range(nk - 1):
        total = total + far_b[k]
    rows_b[...] = total / scale_a
    gather_start(25, rows_b, block_b.at[1])
    inverse = invert(system, half)
    gather_on(25, block_b.at[1])
    raw_a_scaled = raw_a / scale_a
    new_a[...] = jnp.where(core == 0, raw_a_scaled[0:4], raw_a_scaled[4:8])
    per_scale_a = 1.0 / scale_a
    for m in range(members):
        contracted[m] = contracted[m] * per_scale_a
    raw_b_own = dot(rows_b[...], inverse)
    gather_end(25)

    raw_b = dot(gathered(block_b.at[1]), inverse)
    gram_start(2, raw_b, True)
    sums = jnp.concatenate(
        [jnp.sum(contracted[m] * raw_b, axis=0, keepdims=True) for m in range(members)], axis=0
    )
    out_c[0] = sums[:, 0:128]
    out_c[1] = sums[:, 128:256]
    send_c(16, out_c, in_c, lambda other: other % 2)
    gram_middle(2, True)
    arrived(16)
    half_c[...] = sum_of(in_c)
    send_all_z(17, half_c, ring_c)
    gram = gram_of(2)
    scale_b, scale_b_down = scales(gram, wide_b * nc)
    system[...] = gram_c[...] * (gram / (scale_b * scale_b_down))
    new_b[...] = raw_b_own / scale_b

    def half_known():
        arrived(17)
        side_c[core] = sum_of(ring_c)
        copy(15, side_c.at[core], side_c.at[core], (z, c + 1 - 2 * core)).start()
        over(15, side_c.at[0])

    inverse = invert(system, half, half_known)
    arrived(15)
    new_c[...] = dot(jnp.concatenate([side_c[0], side_c[1]], axis=1) / scale_b, inverse)
    for which, whole in totals.items():
        copy(which, whole, whole, (z, c)).wait_send()


def solution(mesh):
    nz, nc = mesh.shape["row"], mesh.shape["col"]
    nq, nk = nc // 2, nz // 4

    def on_device(tensor, factor_b, factor_c):
        members, wide_a, wide_b = tensor.shape
        deep_b, rank = factor_b.shape
        part = rank // nc
        memory = [
            tensor.shape,
            factor_b.shape,
            factor_c.shape,
            (wide_b, members * wide_a),
            (rank, rank),
            (2, 4, nk, deep_b, rank),
            (3, nc, part, rank),
            (3, nc, part, rank),
            (3, part, rank),
            (3, nc, part, rank),
            (nq, 8, rank),
            (nc, 8, rank),
            (8, rank),
            (nz, 8, rank),
            (nq, 8, rank),
            (members, wide_b, rank),
            (4, nk, deep_b, rank),
            (3, nk, deep_b, rank),
            (nk, deep_b, rank),
            (max(nk - 1, 1), deep_b, rank),
            (deep_b, rank),
            (2, members, 128),
            (nc, members, 128),
            (members, 128),
            (nz, members, 128),
            (2, members, 128),
            (rank, rank),
            (128, 128),
        ]
        return pl.pallas_call(
            functools.partial(sweep, nz, nc),
            out_shape=(
                jax.ShapeDtypeStruct((wide_a // nc, rank), f32),
                jax.ShapeDtypeStruct((deep_b, rank), f32),
                jax.ShapeDtypeStruct((members, rank), f32),
            ),
            in_specs=[pl.BlockSpec(memory_space=pltpu.HBM)] * 3,
            out_specs=tuple([pl.BlockSpec(memory_space=pltpu.VMEM)] * 3),
            scratch_shapes=[pltpu.VMEM(shape, f32) for shape in memory]
            + [pltpu.SemaphoreType.DMA((EXCHANGES,)), pltpu.SemaphoreType.DMA((EXCHANGES,))]
            + [pltpu.SemaphoreType.DMA((3,))],
            compiler_params=pltpu.CompilerParams(
                collective_id=0, has_side_effects=True, vmem_limit_bytes=40 * 1024 * 1024
            ),
        )(tensor, factor_b, factor_c)

    return jax.shard_map(
        on_device,
        mesh=mesh,
        in_specs=(P(None, "row", "col"), P("row", "col"), P()),
        out_specs=(P(("row", "col"), None), P("row", "col"), P()),
        check_vma=False,
    )
```

```python
import functools

import jax
import jax.numpy as jnp
from jax import lax
from jax.experimental import pallas as pl
from jax.experimental.pallas import tpu as pltpu
from jax.sharding import PartitionSpec as P

f32 = jnp.float32
bf16 = jnp.bfloat16
highest = lax.Precision.HIGHEST
epsilon = 1e-06
EXCHANGES = 36
MESH = pl.DeviceIdType.MESH


def dot(left, right):
    return jnp.dot(left, right, precision=highest, preferred_element_type=f32)


def lane_of(tile, index):
    return jnp.take_along_axis(tile, jnp.full(tile.shape, index, jnp.int32), axis=1)


def row_of(tile, k):
    return jnp.broadcast_to(tile[k : k + 1], tile.shape)


def added(parts):
    while len(parts) > 1:
        parts = [a + b for a, b in zip(parts[::2], parts[1::2])] + parts[len(parts) & ~1 :]
    return parts[0]


def pivot_panel(tile, p):
    lane = lax.broadcasted_iota(jnp.int32, (8, 128), 1)
    sub = lax.broadcasted_iota(jnp.int32, (8, 128), 0)
    d = [lane_of(tile, p * 8 + k) for k in range(8)]
    for j in range(8):
        here = sub == j
        c = jnp.where(here, -1.0, d[j])
        products = [None if k == j else c * row_of(d[k], j) for k in range(8)]
        r = 1.0 / row_of(d[j], j)
        d = [-c * r if k == j else jnp.where(here, 0.0, d[k]) - products[k] * r for k in range(8)]
    rows = jnp.where(lane // 8 == p, jnp.where(lane % 8 == sub, 1.0, 0.0), tile)
    return added([d[k] * row_of(rows, k) for k in range(8)])


def cleared(tile, p, pivot):
    lane = lax.broadcasted_iota(jnp.int32, (8, 128), 1)
    return jnp.where(lane // 8 == p, 0.0, tile) - added(
        [lane_of(tile, p * 8 + k) * row_of(pivot, k) for k in range(8)]
    )


def thirds(x):
    high = x.astype(bf16).astype(f32)
    rest = x - high
    middle = rest.astype(bf16).astype(f32)
    return high, middle, rest - middle


def outer(left, right):
    lh, lm, ll = thirds(left)
    rh, rm, rl = thirds(right)
    lhs = jnp.concatenate([lh, lh, lm, lh, ll, lm], axis=0).astype(bf16)
    rhs = jnp.concatenate([rh, rm, rh, rl, rh, rm], axis=0).astype(bf16)
    return lax.dot_general(lhs, rhs, (((0,), (0,)), ((), ())), preferred_element_type=f32)


def invert_half(t):
    n = t.shape[0] // 8
    lane = lax.broadcasted_iota(jnp.int32, (8, 128), 1)
    lanes = lax.broadcasted_iota(jnp.int32, (128, 128), 1)

    def step(p, tile, pivot, last):
        if not last:
            ahead = t[pl.ds(pl.multiple_of((p + 1) * 8, 8), 8), :]
            tile_next = cleared(ahead, p, pivot)
            pivot_next = pivot_panel(tile_next, p + 1)
        update = outer(jnp.where(lane < 8 * p, -tile, tile), pivot)
        t[...] = jnp.where(lanes // 8 == p, 0.0, t[...]) - update
        t[pl.ds(pl.multiple_of(p * 8, 8), 8), :] = pivot
        return None if last else (tile_next, pivot_next)

    first = t[0:8, :]
    held = lax.fori_loop(
        0, n - 1, lambda p, v: step(p, *v, False), (first, pivot_panel(first, 0)), unroll=15
    )
    step(n - 1, *held, True)


def between_halves(system, t, first, right, down):
    first[...] = t[...]
    right[...] = dot(t[...], system[0:128, 128:256])
    down[...] = dot(system[128:256, 0:128], t[...])
    t[...] = system[128:256, 128:256] - dot(system[128:256, 0:128], right[...])


def after_halves(t, first, right, down, inverse):
    d = t[...]
    v, vt = dot(right[...], d), dot(d, down[...])
    inverse[0:128, 0:128] = first[...] + dot(v, down[...])
    inverse[0:128, 128:256] = -v
    inverse[128:256, 0:128] = -vt
    inverse[128:256, 128:256] = d


def dot_first(left, right):
    return lax.dot_general(
        left, right, (((0,), (0,)), ((), ())), precision=highest, preferred_element_type=f32
    )


def sweep(
    nz, nc, tensor_in, factor_b_in, factor_c_in, new_a, new_b, new_c,
    tensor, factor_b, factor_c, tensor_t, gram_c, block_b, partial, landed, owned, grams,
    out_m, in_m, rows_m, rows_a, ring_m, block_m, contracted, out_b, near_b, part_b, far_b, rows_b,
    out_c, in_c, half_c, ring_c, side_c, system, half, first, right, down, inverse, scale_a, scale_b, sent, received, loaded,
):
    nq, nk = nc // 2, nz // 4
    z, c = lax.axis_index("row"), lax.axis_index("col")
    q, core = c // 2, c % 2
    class_z, place_z = z % 4, z // 4

    barrier = pltpu.get_barrier_semaphore()
    for k in sorted(range(1, nz), key=lambda k: -min(k, nz - k)):
        pl.semaphore_signal(barrier, inc=1, device_id=(lax.rem(z + k, nz), c), device_id_type=MESH)
    for k in range(1, nc):
        pl.semaphore_signal(barrier, inc=1, device_id=(z, lax.rem(c + k, nc)), device_id_type=MESH)
    loads = [
        pltpu.make_async_copy(src, dst, loaded.at[i])
        for i, (src, dst) in enumerate(((factor_b_in, factor_b), (tensor_in, tensor), (factor_c_in, factor_c)))
    ]
    for load in loads:
        load.start()
    members, wide_a, wide_b = tensor.shape
    rank = factor_b.shape[1]
    pl.semaphore_wait(barrier, nz - 1 + nc - 1)

    def copy(which, src, dst, to):
        return pltpu.make_async_remote_copy(
            src_ref=src, dst_ref=dst, send_sem=sent.at[which], recv_sem=received.at[which],
            device_id=to, device_id_type=MESH,
        )

    totals = {}

    def hops(k):
        return -(min(k % 4, 4 - k % 4) + min(k // 4, 4 - k // 4))

    def view(place):
        return place[0].at[place[1:]] if isinstance(place, tuple) else place

    def over(which, place, *blocks):
        totals[which] = lambda: view(place).at[blocks]

    def arrived(which, offset=0):
        if which in totals:
            whole = totals[which]()
            copy(which + offset, whole, whole, (z, c)).wait_recv()

    def left(which):
        whole = totals[which]()
        copy(which, whole, whole, (z, c)).wait_send()

    def send_all_z(which, src, dst):
        for k in sorted(range(1, nz), key=lambda k: -min(k, nz - k)):
            copy(which, src, dst.at[z], (lax.rem(z + k, nz), c)).start()
        over(which, dst, pl.ds(0, nz - 1))
        dst[z] = src[...]

    def send_q(which, src, place, scatter=False):
        dst = view(place)
        for k in sorted(range(1, nq), key=hops):
            other = lax.rem(q + k, nq)
            copy(which, src.at[2 * other + core] if scatter else src, dst.at[q], (z, 2 * other + core)).start()
        if nq > 1:
            over(which, place, pl.ds(0, nq - 1))
        dst[q] = src[c] if scatter else src[...]

    def send_c(which, src, place, pick=None):
        dst = view(place)
        for k in sorted(range(1, nc), key=lambda k: hops(k // 2)):
            other = lax.rem(c + k, nc)
            copy(which, src.at[pick(other)] if pick else src, dst.at[c], (z, other)).start()
        over(which, place, pl.ds(0, nc - 1))
        dst[c] = src[pick(c)] if pick else src[...]

    def sum_of(ref):
        total = ref[0]
        for k in range(1, ref.shape[0]):
            total = total + ref[k]
        return total

    far = sorted(range(1, nk), key=lambda k: -min(k, nk - k))

    def to_near(which, block):
        for k in (2, 1, nz - 1):
            copy(which, block, block, (lax.rem(z + k, nz), c)).start()

    def gather_start(which, src, place):
        dst = view(place)
        for k in far:
            copy(which + k, src, dst.at[class_z, place_z], (lax.rem(z + 4 * k, nz), c)).start()
            over(which + k, place, 0, 0)
        dst[class_z, place_z] = src[...]
        to_near(which, dst.at[class_z, place_z])
        over(which, place, pl.ds(0, 3), 0)

    def gather_on(which, place):
        dst = view(place)
        for k in reversed(far):
            arrived(which + k)
            to_near(which + nk - 1 + k, dst.at[class_z, lax.rem(place_z + nk - k, nk)])
            over(which + nk - 1 + k, place, pl.ds(0, 3), 0)

    def gather_end(which):
        arrived(which)
        for k in reversed(far):
            arrived(which + nk - 1 + k)

    def gathered(ref):
        return jnp.concatenate([ref[k % 4, k // 4] for k in range(nz)], axis=0)

    def scatter_near(which, src, dst, place):
        for slot, k in enumerate((1, nz - 1, 2)):
            other = lax.rem(z + k, nz)
            copy(which + place, src.at[lax.rem(z + k, 4), place], dst.at[slot, place], (other, c)).start()

    def scatter_far(which, src, dst, k):
        place = lax.rem(place_z + k, nk)
        copy(which, src.at[place], dst.at[k - 1], (lax.rem(z + 4 * k, nz), c)).start()

    part = rank // nc

    def gram_start(turn, block, both):
        partial[turn] = dot_first(block, block).reshape(nc, part, rank)
        if both:
            send_c(3 * turn, partial.at[turn], (landed, turn), lambda other: other)
        else:
            send_q(3 * turn, partial.at[turn], (landed, turn, pl.ds(0, nq)), True)

    def gram_middle(turn, both):
        arrived(3 * turn)
        owned[turn] = sum_of(landed.at[turn] if both else landed.at[turn, pl.ds(0, nq)])
        send_c(3 * turn + 1, owned.at[turn], (grams, turn))

    def gram_of(turn):
        arrived(3 * turn + 1)
        return grams[turn].reshape(rank, rank)

    def scales(gram, count):
        one = lax.broadcasted_iota(jnp.int32, gram.shape, 0) == lax.broadcasted_iota(jnp.int32, gram.shape, 1)
        diagonal = jnp.where(one, gram, 0.0)
        return (
            jnp.sqrt(jnp.sum(diagonal, axis=0, keepdims=True) / count + epsilon),
            jnp.sqrt(jnp.sum(diagonal, axis=1, keepdims=True) / count + epsilon),
        )

    def stage(i, carry):
        @pl.when(i == 0)
        def _():
            loads[0].wait()
            gather_start(18, factor_b, (block_b, 0))
            loads[1].wait()
            loads[2].wait()
            for m in range(members):
                tensor_t[:, m * wide_a : (m + 1) * wide_a] = jnp.transpose(tensor[m])
            by_row = factor_c[...]
            gram_c[...] = dot_first(by_row, by_row)
            gather_on(18, (block_b, 0))
            gather_end(18)
            whole_b = gathered(block_b.at[0])
            gram_start(0, whole_b, True)
            products = dot(tensor[...].reshape(members * wide_a, wide_b), whole_b).reshape(members, wide_a, rank)
            sums = products[0] * by_row[0:1]
            for m in range(1, members):
                sums = sums + products[m] * by_row[m : m + 1]
            out_m[...] = sums.reshape(nq, 8, rank)
            send_c(9, out_m, in_m, lambda other: other // 2)
            gram_middle(0, True)
            arrived(9)
            rows_m[...] = sum_of(in_m)
            send_all_z(10, rows_m, ring_m)
            send_q(11, rows_m, block_m)
            system[...] = gram_of(0) * gram_c[...]
            half[...] = system[0:128, 0:128]

        @pl.when(jnp.logical_and(i > 0, i % 2 == 0))
        def _():
            after_halves(half, first, right, down, inverse)

        @pl.when(i == 2)
        def _():
            arrived(11)
            by_row = factor_c[...]
            whole_a = dot(block_m[...].reshape(wide_a, rank), inverse[...])
            weighted = jnp.concatenate([whole_a * by_row[m : m + 1] for m in range(members)], axis=0)
            deep = wide_b // nk
            for k in far + [0]:
                place = lax.rem(place_z + k, nk)
                rows = pl.ds(pl.multiple_of(place * deep, 8), deep)
                out_b[:, place] = dot(tensor_t[rows, :], weighted).reshape(4, -1, rank)
                scatter_near(32, out_b, near_b, place)
            for k in range(nk):
                over(32 + k, near_b, pl.ds(0, 3), 0)
            arrived(10)
            gram_start(1, dot(ring_m[...].reshape(nz * 8, rank), inverse[...]), False)
            for m in range(members):
                contracted[m] = dot(tensor_t[:, m * wide_a : (m + 1) * wide_a], whole_a)
            rows_a[...] = dot(rows_m[...], inverse[...])
            for k in far + [0]:
                place = lax.rem(place_z + k, nk)
                arrived(32, place)
                part_b[place] = (out_b[class_z, place] + near_b[0, place]) + (near_b[1, place] + near_b[2, place])
                if k:
                    scatter_far(13, part_b, far_b, k)
            if nk > 1:
                over(13, far_b, pl.ds(0, nk - 1))
            gram_middle(1, False)
            arrived(13)
            total = part_b[place_z]
            for k in range(nk - 1):
                total = total + far_b[k]
            rows_b[...] = total
            gather_start(25, rows_b, (block_b, 1))
            gram = gram_of(1)
            across, along = scales(gram, wide_a * nz)
            scale_a[...] = across
            gram_a = gram / (across * along)
            system[...] = gram_a * gram_c[...]
            gram_c[...] = gram_a
            own = rows_a[...] / across
            new_a[...] = jnp.where(core == 0, own[0:4], own[4:8])
            half[...] = system[0:128, 0:128]

        @pl.when(i == 3)
        def _():
            gather_on(25, (block_b, 1))

        @pl.when(i == 4)
        def _():
            per_scale_a = 1.0 / scale_a[...]
            for m in range(members):
                contracted[m] = contracted[m] * per_scale_a
            raw_b_own = dot(rows_b[...] * per_scale_a, inverse[...])
            gather_end(25)

            raw_b = dot(gathered(block_b.at[1]) * per_scale_a, inverse[...])
            gram_start(2, raw_b, True)
            sums = jnp.concatenate(
                [jnp.sum(contracted[m] * raw_b, axis=0, keepdims=True) for m in range(members)], axis=0
            )
            out_c[0] = sums[:, 0:128]
            out_c[1] = sums[:, 128:256]
            send_c(16, out_c, in_c, lambda other: other % 2)
            gram_middle(2, True)
            arrived(16)
            half_c[...] = sum_of(in_c)
            send_all_z(17, half_c, ring_c)
            gram = gram_of(2)
            across, along = scales(gram, wide_b * nc)
            scale_b[...] = across
            system[...] = gram_c[...] * (gram / (across * along))
            new_b[...] = raw_b_own / across
            half[...] = system[0:128, 0:128]

        @pl.when(i == 5)
        def _():
            arrived(17)
            side_c[core] = sum_of(ring_c)
            copy(15, side_c.at[core], side_c.at[core], (z, c + 1 - 2 * core)).start()
            over(15, side_c, 0)

        @pl.when(i % 2 == 1)
        def _():
            between_halves(system, half, first, right, down)

        invert_half(half)
        return carry

    lax.fori_loop(0, 6, stage, 0)
    after_halves(half, first, right, down, inverse)
    arrived(15)
    new_c[...] = dot(jnp.concatenate([side_c[0], side_c[1]], axis=1) / scale_b[...], inverse[...])
    for which in totals:
        left(which)


def solution(mesh):
    nz, nc = mesh.shape["row"], mesh.shape["col"]
    nq, nk = nc // 2, nz // 4

    def on_device(tensor, factor_b, factor_c):
        members, wide_a, wide_b = tensor.shape
        deep_b, rank = factor_b.shape
        part = rank // nc
        memory = [
            tensor.shape,
            factor_b.shape,
            factor_c.shape,
            (wide_b, members * wide_a),
            (rank, rank),
            (2, 4, nk, deep_b, rank),
            (3, nc, part, rank),
            (3, nc, part, rank),
            (3, part, rank),
            (3, nc, part, rank),
            (nq, 8, rank),
            (nc, 8, rank),
            (8, rank),
            (8, rank),
            (nz, 8, rank),
            (nq, 8, rank),
            (members, wide_b, rank),
            (4, nk, deep_b, rank),
            (3, nk, deep_b, rank),
            (nk, deep_b, rank),
            (max(nk - 1, 1), deep_b, rank),
            (deep_b, rank),
            (2, members, 128),
            (nc, members, 128),
            (members, 128),
            (nz, members, 128),
            (2, members, 128),
            (rank, rank),
            (128, 128),
            (128, 128),
            (128, 128),
            (128, 128),
            (rank, rank),
            (1, rank),
            (1, rank),
        ]
        return pl.pallas_call(
            functools.partial(sweep, nz, nc),
            out_shape=(
                jax.ShapeDtypeStruct((wide_a // nc, rank), f32),
                jax.ShapeDtypeStruct((deep_b, rank), f32),
                jax.ShapeDtypeStruct((members, rank), f32),
            ),
            in_specs=[pl.BlockSpec(memory_space=pltpu.HBM)] * 3,
            out_specs=tuple([pl.BlockSpec(memory_space=pltpu.VMEM)] * 3),
            scratch_shapes=[pltpu.VMEM(shape, f32) for shape in memory]
            + [pltpu.SemaphoreType.DMA((EXCHANGES,)), pltpu.SemaphoreType.DMA((EXCHANGES,))]
            + [pltpu.SemaphoreType.DMA((3,))],
            compiler_params=pltpu.CompilerParams(
                collective_id=0, has_side_effects=True, vmem_limit_bytes=40 * 1024 * 1024
            ),
        )(tensor, factor_b, factor_c)

    return jax.shard_map(
        on_device,
        mesh=mesh,
        in_specs=(P(None, "row", "col"), P("row", "col"), P()),
        out_specs=(P(("row", "col"), None), P("row", "col"), P()),
        check_vma=False,
    )
```

```python
import functools

import jax
import jax.numpy as jnp
from jax import lax
from jax.experimental import pallas as pl
from jax.experimental.pallas import tpu as pltpu
from jax.sharding import PartitionSpec as P

f32 = jnp.float32
bf16 = jnp.bfloat16
highest = lax.Precision.HIGHEST
epsilon = 1e-06
EXCHANGES = 52
MESH = pl.DeviceIdType.MESH


def dot(left, right):
    return jnp.dot(left, right, precision=highest, preferred_element_type=f32)


def lane_of(tile, index):
    return jnp.take_along_axis(tile, jnp.full(tile.shape, index, jnp.int32), axis=1)


def row_of(tile, k):
    return jnp.broadcast_to(tile[k : k + 1], tile.shape)


def added(parts):
    while len(parts) > 1:
        parts = [a + b for a, b in zip(parts[::2], parts[1::2])] + parts[len(parts) & ~1 :]
    return parts[0]


def pivot_panel(tile, p):
    lane = lax.broadcasted_iota(jnp.int32, (8, 128), 1)
    sub = lax.broadcasted_iota(jnp.int32, (8, 128), 0)
    d = [lane_of(tile, p * 8 + k) for k in range(8)]
    for j in range(8):
        here = sub == j
        c = jnp.where(here, -1.0, d[j])
        products = [None if k == j else c * row_of(d[k], j) for k in range(8)]
        r = 1.0 / row_of(d[j], j)
        d = [-c * r if k == j else jnp.where(here, 0.0, d[k]) - products[k] * r for k in range(8)]
    rows = jnp.where(lane // 8 == p, jnp.where(lane % 8 == sub, 1.0, 0.0), tile)
    return added([d[k] * row_of(rows, k) for k in range(8)])


def cleared(tile, p, pivot):
    lane = lax.broadcasted_iota(jnp.int32, (8, 128), 1)
    return jnp.where(lane // 8 == p, 0.0, tile) - added(
        [lane_of(tile, p * 8 + k) * row_of(pivot, k) for k in range(8)]
    )


def thirds(x):
    high = x.astype(bf16).astype(f32)
    rest = x - high
    middle = rest.astype(bf16).astype(f32)
    return high, middle, rest - middle


def outer(left, right):
    lh, lm, ll = thirds(left)
    rh, rm, rl = thirds(right)
    lhs = jnp.concatenate([lh, lh, lm, lh, ll, lm], axis=0).astype(bf16)
    rhs = jnp.concatenate([rh, rm, rh, rl, rh, rm], axis=0).astype(bf16)
    return lax.dot_general(lhs, rhs, (((0,), (0,)), ((), ())), preferred_element_type=f32)


def invert_half(t):
    n = t.shape[0] // 8
    lane = lax.broadcasted_iota(jnp.int32, (8, 128), 1)
    lanes = lax.broadcasted_iota(jnp.int32, (128, 128), 1)

    def step(p, tile, pivot, last):
        if not last:
            ahead = t[pl.ds(pl.multiple_of((p + 1) * 8, 8), 8), :]
            tile_next = cleared(ahead, p, pivot)
            pivot_next = pivot_panel(tile_next, p + 1)
        update = outer(jnp.where(lane < 8 * p, -tile, tile), pivot)
        t[...] = jnp.where(lanes // 8 == p, 0.0, t[...]) - update
        t[pl.ds(pl.multiple_of(p * 8, 8), 8), :] = pivot
        return None if last else (tile_next, pivot_next)

    first = t[0:8, :]
    held = lax.fori_loop(
        0, n - 1, lambda p, v: step(p, *v, False), (first, pivot_panel(first, 0)), unroll=15
    )
    step(n - 1, *held, True)


def between_halves(system, t, first, right, down):
    first[...] = t[...]
    right[...] = dot(t[...], system[0:128, 128:256])
    down[...] = dot(system[128:256, 0:128], t[...])
    t[...] = system[128:256, 128:256] - dot(system[128:256, 0:128], right[...])


def after_halves(t, first, right, down, inverse):
    d = t[...]
    v, vt = dot(right[...], d), dot(d, down[...])
    inverse[0:128, 0:128] = first[...] + dot(v, down[...])
    inverse[0:128, 128:256] = -v
    inverse[128:256, 0:128] = -vt
    inverse[128:256, 128:256] = d


def dot_first(left, right):
    return lax.dot_general(
        left, right, (((0,), (0,)), ((), ())), precision=highest, preferred_element_type=f32
    )


def sweep(
    nz, nc, tensor_in, factor_b_in, factor_c_in, new_a, new_b, new_c,
    tensor, factor_b, factor_c, tensor_t, gram_c, block_b, partial, landed, owned, grams,
    out_m, in_m, rows_m, rows_a, ring_m, block_m, contracted, out_b, near_b, part_b, far_b, rows_b, raw_b_own,
    out_c, in_c, half_c, ring_c, side_c, system, half, first, right, down, inverse, scale_a, scale_b, sent, received, loaded,
):
    nq, nk = nc // 2, nz // 4
    z, c = lax.axis_index("row"), lax.axis_index("col")
    q, core = c // 2, c % 2
    class_z, place_z = z % 4, z // 4

    barrier = pltpu.get_barrier_semaphore()
    for k in sorted(range(1, nz), key=lambda k: -min(k, nz - k)):
        pl.semaphore_signal(barrier, inc=1, device_id=(lax.rem(z + k, nz), c), device_id_type=MESH)
    for k in range(1, nc):
        pl.semaphore_signal(barrier, inc=1, device_id=(z, lax.rem(c + k, nc)), device_id_type=MESH)
    loads = [
        pltpu.make_async_copy(src, dst, loaded.at[i])
        for i, (src, dst) in enumerate(((factor_b_in, factor_b), (tensor_in, tensor), (factor_c_in, factor_c)))
    ]
    for load in loads:
        load.start()
    members, wide_a, wide_b = tensor.shape
    rank = factor_b.shape[1]
    pl.semaphore_wait(barrier, nz - 1 + nc - 1)

    def copy(which, src, dst, to):
        return pltpu.make_async_remote_copy(
            src_ref=src, dst_ref=dst, send_sem=sent.at[which], recv_sem=received.at[which],
            device_id=to, device_id_type=MESH,
        )

    totals = {}

    def hops(k):
        return -(min(k % 4, 4 - k % 4) + min(k // 4, 4 - k // 4))

    def view(place):
        return place[0].at[place[1:]] if isinstance(place, tuple) else place

    def over(which, place, *blocks):
        totals[which] = lambda: view(place).at[blocks]

    def arrived(which, offset=0):
        if which in totals:
            whole = totals[which]()
            copy(which + offset, whole, whole, (z, c)).wait_recv()

    def left(which):
        whole = totals[which]()
        copy(which, whole, whole, (z, c)).wait_send()

    def send_all_z(which, src, dst):
        for k in sorted(range(1, nz), key=lambda k: -min(k, nz - k)):
            copy(which, src, dst.at[z], (lax.rem(z + k, nz), c)).start()
        over(which, dst, pl.ds(0, nz - 1))
        dst[z] = src[...]

    def send_q(which, src, place, scatter=False):
        dst = view(place)
        for k in sorted(range(1, nq), key=hops):
            other = lax.rem(q + k, nq)
            copy(which, src.at[2 * other + core] if scatter else src, dst.at[q], (z, 2 * other + core)).start()
        if nq > 1:
            over(which, place, pl.ds(0, nq - 1))
        dst[q] = src[c] if scatter else src[...]

    def send_c(which, src, place, pick=None):
        dst = view(place)
        for k in sorted(range(1, nc), key=lambda k: hops(k // 2)):
            other = lax.rem(c + k, nc)
            copy(which, src.at[pick(other)] if pick else src, dst.at[c], (z, other)).start()
        over(which, place, pl.ds(0, nc - 1))
        dst[c] = src[pick(c)] if pick else src[...]

    def sum_of(ref):
        total = ref[0]
        for k in range(1, ref.shape[0]):
            total = total + ref[k]
        return total

    far = sorted(range(1, nk), key=lambda k: -min(k, nk - k))

    def to_near(which, block):
        for k in (2, 1, nz - 1):
            copy(which, block, block, (lax.rem(z + k, nz), c)).start()

    def gather_start(which, src, place):
        dst = view(place)
        for k in far:
            copy(which + k, src, dst.at[class_z, place_z], (lax.rem(z + 4 * k, nz), c)).start()
            over(which + k, place, 0, 0)
        dst[class_z, place_z] = src[...]
        to_near(which, dst.at[class_z, place_z])
        over(which, place, pl.ds(0, 3), 0)

    def gather_on(which, place):
        dst = view(place)
        for k in reversed(far):
            arrived(which + k)
            to_near(which + nk - 1 + k, dst.at[class_z, lax.rem(place_z + nk - k, nk)])
            over(which + nk - 1 + k, place, pl.ds(0, 3), 0)

    def gather_end(which):
        arrived(which)
        for k in reversed(far):
            arrived(which + nk - 1 + k)

    def gathered(ref):
        return jnp.concatenate([ref[k % 4, k // 4] for k in range(nz)], axis=0)

    def scatter_near(which, src, dst, place):
        for slot, k in enumerate((1, nz - 1, 2)):
            other = lax.rem(z + k, nz)
            copy(which + place, src.at[lax.rem(z + k, 4), place], dst.at[slot, place], (other, c)).start()

    def scatter_far(which, src, dst, k):
        place = lax.rem(place_z + k, nk)
        copy(which, src.at[place], dst.at[k - 1], (lax.rem(z + 4 * k, nz), c)).start()

    part = rank // nc

    def gram_start(turn, block, both):
        whole = dot_first(block, block)
        for side in range(2):
            partial[turn, side] = whole[:, 128 * side : 128 * side + 128].reshape(nc, part, 128)
            if both:
                send_c(40 + 4 * turn + side, partial.at[turn, side], (landed, turn, side), lambda other: other)
            else:
                send_q(40 + 4 * turn + side, partial.at[turn, side], (landed, turn, side, pl.ds(0, nq)), True)

    def gram_middle(turn, both):
        for side in range(2):
            arrived(40 + 4 * turn + side)
            owned[turn, side] = sum_of(landed.at[turn, side] if both else landed.at[turn, side, pl.ds(0, nq)])
            send_c(42 + 4 * turn + side, owned.at[turn, side], (grams, turn, side))

    def leading(turn):
        arrived(42 + 4 * turn)
        return grams[turn, 0, 0 : nc // 2].reshape(128, 128)

    def gram_of(turn):
        arrived(43 + 4 * turn)
        return jnp.concatenate([grams[turn, side].reshape(rank, 128) for side in range(2)], axis=1)

    def scales(gram, count):
        one = lax.broadcasted_iota(jnp.int32, gram.shape, 0) == lax.broadcasted_iota(jnp.int32, gram.shape, 1)
        diagonal = jnp.where(one, gram, 0.0)
        return (
            jnp.sqrt(jnp.sum(diagonal, axis=0, keepdims=True) / count + epsilon),
            jnp.sqrt(jnp.sum(diagonal, axis=1, keepdims=True) / count + epsilon),
        )

    def stage(i, carry):
        @pl.when(i == 0)
        def _():
            loads[0].wait()
            gather_start(18, factor_b, (block_b, 0))
            loads[1].wait()
            loads[2].wait()
            for m in range(members):
                tensor_t[:, m * wide_a : (m + 1) * wide_a] = jnp.transpose(tensor[m])
            by_row = factor_c[...]
            gram_c[...] = dot_first(by_row, by_row)
            gather_on(18, (block_b, 0))
            gather_end(18)
            whole_b = gathered(block_b.at[0])
            gram_start(0, whole_b, True)
            products = dot(tensor[...].reshape(members * wide_a, wide_b), whole_b).reshape(members, wide_a, rank)
            sums = products[0] * by_row[0:1]
            for m in range(1, members):
                sums = sums + products[m] * by_row[m : m + 1]
            out_m[...] = sums.reshape(nq, 8, rank)
            send_c(9, out_m, in_m, lambda other: other // 2)
            gram_middle(0, True)
            arrived(9)
            rows_m[...] = sum_of(in_m)
            send_all_z(10, rows_m, ring_m)
            send_q(11, rows_m, block_m)
            half[...] = leading(0) * gram_c[0:128, 0:128]

        @pl.when(i == 1)
        def _():
            system[...] = gram_of(0) * gram_c[...]

        @pl.when(jnp.logical_and(i > 0, i % 2 == 0))
        def _():
            after_halves(half, first, right, down, inverse)

        @pl.when(i == 2)
        def _():
            arrived(11)
            by_row = factor_c[...]
            whole_a = dot(block_m[...].reshape(wide_a, rank), inverse[...])
            weighted = jnp.concatenate([whole_a * by_row[m : m + 1] for m in range(members)], axis=0)
            deep = wide_b // nk
            for k in far + [0]:
                place = lax.rem(place_z + k, nk)
                rows = pl.ds(pl.multiple_of(place * deep, 8), deep)
                out_b[:, place] = dot(tensor_t[rows, :], weighted).reshape(4, -1, rank)
                scatter_near(32, out_b, near_b, place)
            for k in range(nk):
                over(32 + k, near_b, pl.ds(0, 3), 0)
            arrived(10)
            gram_start(1, dot(ring_m[...].reshape(nz * 8, rank), inverse[...]), False)
            for m in range(members):
                contracted[m] = dot(tensor_t[:, m * wide_a : (m + 1) * wide_a], whole_a)
            rows_a[...] = dot(rows_m[...], inverse[...])
            for k in far + [0]:
                place = lax.rem(place_z + k, nk)
                arrived(32, place)
                part_b[place] = (out_b[class_z, place] + near_b[0, place]) + (near_b[1, place] + near_b[2, place])
                if k:
                    scatter_far(13, part_b, far_b, k)
            if nk > 1:
                over(13, far_b, pl.ds(0, nk - 1))
            gram_middle(1, False)
            arrived(13)
            total = part_b[place_z]
            for k in range(nk - 1):
                total = total + far_b[k]
            rows_b[...] = total
            gather_start(25, rows_b, (block_b, 1))
            gram = leading(1)
            across, along = scales(gram, wide_a * nz)
            half[...] = gram / (across * along) * gram_c[0:128, 0:128]

        @pl.when(i == 3)
        def _():
            gram = gram_of(1)
            across, along = scales(gram, wide_a * nz)
            scale_a[...] = across
            gram_a = gram / (across * along)
            system[...] = gram_a * gram_c[...]
            gram_c[...] = gram_a
            own = rows_a[...] / across
            new_a[...] = jnp.where(core == 0, own[0:4], own[4:8])
            gather_on(25, (block_b, 1))

        @pl.when(i == 4)
        def _():
            per_scale_a = 1.0 / scale_a[...]
            for m in range(members):
                contracted[m] = contracted[m] * per_scale_a
            raw_b_own[...] = dot(rows_b[...] * per_scale_a, inverse[...])
            gather_end(25)

            raw_b = dot(gathered(block_b.at[1]) * per_scale_a, inverse[...])
            gram_start(2, raw_b, True)
            sums = jnp.concatenate(
                [jnp.sum(contracted[m] * raw_b, axis=0, keepdims=True) for m in range(members)], axis=0
            )
            out_c[0] = sums[:, 0:128]
            out_c[1] = sums[:, 128:256]
            send_c(16, out_c, in_c, lambda other: other % 2)
            gram_middle(2, True)
            arrived(16)
            half_c[...] = sum_of(in_c)
            send_all_z(17, half_c, ring_c)
            gram = leading(2)
            across, along = scales(gram, wide_b * nc)
            half[...] = gram_c[0:128, 0:128] * (gram / (across * along))

        @pl.when(i == 5)
        def _():
            gram = gram_of(2)
            across, along = scales(gram, wide_b * nc)
            scale_b[...] = across
            system[...] = gram_c[...] * (gram / (across * along))
            new_b[...] = raw_b_own[...] / across
            arrived(17)
            side_c[core] = sum_of(ring_c)
            copy(15, side_c.at[core], side_c.at[core], (z, c + 1 - 2 * core)).start()
            over(15, side_c, 0)

        @pl.when(i % 2 == 1)
        def _():
            between_halves(system, half, first, right, down)

        invert_half(half)
        return carry

    lax.fori_loop(0, 6, stage, 0)
    after_halves(half, first, right, down, inverse)
    arrived(15)
    new_c[...] = dot(jnp.concatenate([side_c[0], side_c[1]], axis=1) / scale_b[...], inverse[...])
    for which in totals:
        left(which)


def solution(mesh):
    nz, nc = mesh.shape["row"], mesh.shape["col"]
    nq, nk = nc // 2, nz // 4

    def on_device(tensor, factor_b, factor_c):
        members, wide_a, wide_b = tensor.shape
        deep_b, rank = factor_b.shape
        part = rank // nc
        memory = [
            tensor.shape,
            factor_b.shape,
            factor_c.shape,
            (wide_b, members * wide_a),
            (rank, rank),
            (2, 4, nk, deep_b, rank),
            (3, 2, nc, part, 128),
            (3, 2, nc, part, 128),
            (3, 2, part, 128),
            (3, 2, nc, part, 128),
            (nq, 8, rank),
            (nc, 8, rank),
            (8, rank),
            (8, rank),
            (nz, 8, rank),
            (nq, 8, rank),
            (members, wide_b, rank),
            (4, nk, deep_b, rank),
            (3, nk, deep_b, rank),
            (nk, deep_b, rank),
            (max(nk - 1, 1), deep_b, rank),
            (deep_b, rank),
            (deep_b, rank),
            (2, members, 128),
            (nc, members, 128),
            (members, 128),
            (nz, members, 128),
            (2, members, 128),
            (rank, rank),
            (128, 128),
            (128, 128),
            (128, 128),
            (128, 128),
            (rank, rank),
            (1, rank),
            (1, rank),
        ]
        return pl.pallas_call(
            functools.partial(sweep, nz, nc),
            out_shape=(
                jax.ShapeDtypeStruct((wide_a // nc, rank), f32),
                jax.ShapeDtypeStruct((deep_b, rank), f32),
                jax.ShapeDtypeStruct((members, rank), f32),
            ),
            in_specs=[pl.BlockSpec(memory_space=pltpu.HBM)] * 3,
            out_specs=tuple([pl.BlockSpec(memory_space=pltpu.VMEM)] * 3),
            scratch_shapes=[pltpu.VMEM(shape, f32) for shape in memory]
            + [pltpu.SemaphoreType.DMA((EXCHANGES,)), pltpu.SemaphoreType.DMA((EXCHANGES,))]
            + [pltpu.SemaphoreType.DMA((3,))],
            compiler_params=pltpu.CompilerParams(
                collective_id=0, has_side_effects=True, vmem_limit_bytes=40 * 1024 * 1024
            ),
        )(tensor, factor_b, factor_c)

    return jax.shard_map(
        on_device,
        mesh=mesh,
        in_specs=(P(None, "row", "col"), P("row", "col"), P()),
        out_specs=(P(("row", "col"), None), P("row", "col"), P()),
        check_vma=False,
    )
```

```python
import functools

import jax
import jax.numpy as jnp
from jax import lax
from jax.experimental import pallas as pl
from jax.experimental.pallas import tpu as pltpu
from jax.sharding import PartitionSpec as P

f32 = jnp.float32
bf16 = jnp.bfloat16
highest = lax.Precision.HIGHEST
epsilon = 1e-06
EXCHANGES = 52
MESH = pl.DeviceIdType.MESH


def dot(left, right):
    return jnp.dot(left, right, precision=highest, preferred_element_type=f32)


def lane_of(tile, index):
    return jnp.take_along_axis(tile, jnp.full(tile.shape, index, jnp.int32), axis=1)


def row_of(tile, k):
    return jnp.broadcast_to(tile[k : k + 1], tile.shape)


def added(parts):
    while len(parts) > 1:
        parts = [a + b for a, b in zip(parts[::2], parts[1::2])] + parts[len(parts) & ~1 :]
    return parts[0]


def pivot_panel(tile, p):
    lane = lax.broadcasted_iota(jnp.int32, (8, 128), 1)
    sub = lax.broadcasted_iota(jnp.int32, (8, 128), 0)
    d = [lane_of(tile, p * 8 + k) for k in range(8)]
    for j in range(8):
        here = sub == j
        c = jnp.where(here, -1.0, d[j])
        products = [None if k == j else c * row_of(d[k], j) for k in range(8)]
        r = 1.0 / row_of(d[j], j)
        d = [-c * r if k == j else jnp.where(here, 0.0, d[k]) - products[k] * r for k in range(8)]
    rows = jnp.where(lane // 8 == p, jnp.where(lane % 8 == sub, 1.0, 0.0), tile)
    return added([d[k] * row_of(rows, k) for k in range(8)])


def cleared(tile, p, pivot):
    lane = lax.broadcasted_iota(jnp.int32, (8, 128), 1)
    return jnp.where(lane // 8 == p, 0.0, tile) - added(
        [lane_of(tile, p * 8 + k) * row_of(pivot, k) for k in range(8)]
    )


def thirds(x):
    high = x.astype(bf16).astype(f32)
    rest = x - high
    middle = rest.astype(bf16).astype(f32)
    return high, middle, rest - middle


def outer(left, right):
    lh, lm, ll = thirds(left)
    rh, rm, rl = thirds(right)
    lhs = jnp.concatenate([lh, lh, lm, lh, ll, lm], axis=0).astype(bf16)
    rhs = jnp.concatenate([rh, rm, rh, rl, rh, rm], axis=0).astype(bf16)
    return lax.dot_general(lhs, rhs, (((0,), (0,)), ((), ())), preferred_element_type=f32)


def invert_half(t):
    n = t.shape[0] // 8
    lane = lax.broadcasted_iota(jnp.int32, (8, 128), 1)
    lanes = lax.broadcasted_iota(jnp.int32, (128, 128), 1)

    def step(p, tile, pivot, last):
        if not last:
            ahead = t[pl.ds(pl.multiple_of((p + 1) * 8, 8), 8), :]
            tile_next = cleared(ahead, p, pivot)
            pivot_next = pivot_panel(tile_next, p + 1)
        update = outer(jnp.where(lane < 8 * p, -tile, tile), pivot)
        t[...] = jnp.where(lanes // 8 == p, 0.0, t[...]) - update
        t[pl.ds(pl.multiple_of(p * 8, 8), 8), :] = pivot
        return None if last else (tile_next, pivot_next)

    first = t[0:8, :]
    held = lax.fori_loop(
        0, n - 1, lambda p, v: step(p, *v, False), (first, pivot_panel(first, 0)), unroll=15
    )
    step(n - 1, *held, True)


def between_halves(system, t, first, right, down):
    first[...] = t[...]
    right[...] = dot(t[...], system[0:128, 128:256])
    down[...] = dot(system[128:256, 0:128], t[...])
    t[...] = system[128:256, 128:256] - dot(system[128:256, 0:128], right[...])


def after_halves(t, first, right, down, inverse):
    d = t[...]
    v, vt = dot(right[...], d), dot(d, down[...])
    inverse[0:128, 0:128] = first[...] + dot(v, down[...])
    inverse[0:128, 128:256] = -v
    inverse[128:256, 0:128] = -vt
    inverse[128:256, 128:256] = d


def dot_first(left, right):
    return lax.dot_general(
        left, right, (((0,), (0,)), ((), ())), precision=highest, preferred_element_type=f32
    )


def sweep(
    nz, nc, tensor_in, factor_b_in, factor_c_in, new_a, new_b, new_c,
    tensor, factor_b, factor_c, tensor_t, gram_c, block_b, partial, landed, owned, grams,
    out_m, in_m, rows_m, rows_a, ring_m, block_m, contracted, out_b, near_b, part_b, far_b, rows_b, raw_b_own,
    out_c, in_c, half_c, ring_c, side_c, system, half, first, right, down, inverse, scale_a, scale_b, sent, received, loaded,
):
    nq, nk = nc // 2, nz // 4
    z, c = lax.axis_index("row"), lax.axis_index("col")
    q, core = c // 2, c % 2
    class_z, place_z = z % 4, z // 4

    barrier = pltpu.get_barrier_semaphore()
    for k in sorted(range(1, nz), key=lambda k: -min(k, nz - k)):
        pl.semaphore_signal(barrier, inc=1, device_id=(lax.rem(z + k, nz), c), device_id_type=MESH)
    for k in range(1, nc):
        pl.semaphore_signal(barrier, inc=1, device_id=(z, lax.rem(c + k, nc)), device_id_type=MESH)
    loads = [
        pltpu.make_async_copy(src, dst, loaded.at[i])
        for i, (src, dst) in enumerate(((factor_b_in, factor_b), (tensor_in, tensor), (factor_c_in, factor_c)))
    ]
    for load in loads:
        load.start()
    members, wide_a, wide_b = tensor.shape
    rank = factor_b.shape[1]
    pl.semaphore_wait(barrier, nz - 1 + nc - 1)

    def copy(which, src, dst, to):
        return pltpu.make_async_remote_copy(
            src_ref=src, dst_ref=dst, send_sem=sent.at[which], recv_sem=received.at[which],
            device_id=to, device_id_type=MESH,
        )

    totals = {}

    def hops(k):
        return -(min(k % 4, 4 - k % 4) + min(k // 4, 4 - k // 4))

    def view(place):
        return place[0].at[place[1:]] if isinstance(place, tuple) else place

    def over(which, place, *blocks):
        totals[which] = lambda: view(place).at[blocks]

    def arrived(which, offset=0):
        if which in totals:
            whole = totals[which]()
            copy(which + offset, whole, whole, (z, c)).wait_recv()

    def left(which):
        whole = totals[which]()
        copy(which, whole, whole, (z, c)).wait_send()

    def send_all_z(which, src, dst):
        for k in sorted(range(1, nz), key=lambda k: -min(k, nz - k)):
            copy(which, src, dst.at[z], (lax.rem(z + k, nz), c)).start()
        over(which, dst, pl.ds(0, nz - 1))
        dst[z] = src[...]

    def send_q(which, src, place, scatter=False):
        dst = view(place)
        for k in sorted(range(1, nq), key=hops):
            other = lax.rem(q + k, nq)
            copy(which, src.at[2 * other + core] if scatter else src, dst.at[q], (z, 2 * other + core)).start()
        if nq > 1:
            over(which, place, pl.ds(0, nq - 1))
        dst[q] = src[c] if scatter else src[...]

    def send_c(which, src, place, pick=None):
        dst = view(place)
        for k in sorted(range(1, nc), key=lambda k: hops(k // 2)):
            other = lax.rem(c + k, nc)
            copy(which, src.at[pick(other)] if pick else src, dst.at[c], (z, other)).start()
        over(which, place, pl.ds(0, nc - 1))
        dst[c] = src[pick(c)] if pick else src[...]

    def sum_of(ref):
        total = ref[0]
        for k in range(1, ref.shape[0]):
            total = total + ref[k]
        return total

    far = sorted(range(1, nk), key=lambda k: -min(k, nk - k))

    def to_near(which, block):
        for k in (2, 1, nz - 1):
            copy(which, block, block, (lax.rem(z + k, nz), c)).start()

    def gather_start(which, src, place):
        dst = view(place)
        for k in far:
            copy(which + k, src, dst.at[class_z, place_z], (lax.rem(z + 4 * k, nz), c)).start()
            over(which + k, place, 0, 0)
        dst[class_z, place_z] = src[...]
        to_near(which, dst.at[class_z, place_z])
        over(which, place, pl.ds(0, 3), 0)

    def gather_on(which, place):
        dst = view(place)
        for k in reversed(far):
            arrived(which + k)
            to_near(which + nk - 1 + k, dst.at[class_z, lax.rem(place_z + nk - k, nk)])
            over(which + nk - 1 + k, place, pl.ds(0, 3), 0)

    def gather_end(which):
        arrived(which)
        for k in reversed(far):
            arrived(which + nk - 1 + k)

    def gathered(ref):
        return jnp.concatenate([ref[k % 4, k // 4] for k in range(nz)], axis=0)

    def scatter_near(which, src, dst, place):
        for slot, k in enumerate((1, nz - 1, 2)):
            other = lax.rem(z + k, nz)
            copy(which + place, src.at[lax.rem(z + k, 4), place], dst.at[slot, place], (other, c)).start()

    def scatter_far(which, src, dst, k):
        place = lax.rem(place_z + k, nk)
        copy(which, src.at[place], dst.at[k - 1], (lax.rem(z + 4 * k, nz), c)).start()

    part = rank // nc

    def gram_start(turn, block, both):
        whole = dot_first(block, block)
        for side in range(2):
            partial[turn, side] = whole[:, 128 * side : 128 * side + 128].reshape(nc, part, 128)
            if both:
                send_c(40 + 4 * turn + side, partial.at[turn, side], (landed, turn, side), lambda other: other)
            else:
                send_q(40 + 4 * turn + side, partial.at[turn, side], (landed, turn, side, pl.ds(0, nq)), True)

    def gram_middle(turn, both):
        for side in range(2):
            arrived(40 + 4 * turn + side)
            owned[turn, side] = sum_of(landed.at[turn, side] if both else landed.at[turn, side, pl.ds(0, nq)])
            send_c(42 + 4 * turn + side, owned.at[turn, side], (grams, turn, side))

    def leading(turn):
        arrived(42 + 4 * turn)
        return grams[turn, 0, 0 : nc // 2].reshape(128, 128)

    def gram_of(turn):
        arrived(43 + 4 * turn)
        return jnp.concatenate([grams[turn, side].reshape(rank, 128) for side in range(2)], axis=1)

    def scales(gram, count):
        one = lax.broadcasted_iota(jnp.int32, gram.shape, 0) == lax.broadcasted_iota(jnp.int32, gram.shape, 1)
        diagonal = jnp.where(one, gram, 0.0)
        return (
            jnp.sqrt(jnp.sum(diagonal, axis=0, keepdims=True) / count + epsilon),
            jnp.sqrt(jnp.sum(diagonal, axis=1, keepdims=True) / count + epsilon),
        )

    def stage(i, carry):
        @pl.when(i == 0)
        def _():
            loads[0].wait()
            gather_start(18, factor_b, (block_b, 0))
            loads[1].wait()
            loads[2].wait()
            for m in range(members):
                tensor_t[:, m * wide_a : (m + 1) * wide_a] = jnp.transpose(tensor[m])
            by_row = factor_c[...]
            gram_c[...] = dot_first(by_row, by_row)
            gather_on(18, (block_b, 0))
            gather_end(18)
            whole_b = gathered(block_b.at[0])
            gram_start(0, whole_b, True)
            products = dot(tensor[...].reshape(members * wide_a, wide_b), whole_b).reshape(members, wide_a, rank)
            sums = products[0] * by_row[0:1]
            for m in range(1, members):
                sums = sums + products[m] * by_row[m : m + 1]
            out_m[...] = sums.reshape(nq, 8, rank)
            send_c(9, out_m, in_m, lambda other: other // 2)
            gram_middle(0, True)
            arrived(9)
            rows_m[...] = sum_of(in_m)
            send_all_z(10, rows_m, ring_m)
            send_q(11, rows_m, block_m)
            half[...] = leading(0) * gram_c[0:128, 0:128]

        @pl.when(i == 1)
        def _():
            system[...] = gram_of(0) * gram_c[...]

        @pl.when(jnp.logical_and(i > 0, i % 2 == 0))
        def _():
            after_halves(half, first, right, down, inverse)

        @pl.when(i == 2)
        def _():
            arrived(11)
            by_row = factor_c[...]
            whole_a = dot(block_m[...].reshape(wide_a, rank), inverse[...])
            weighted = jnp.concatenate([whole_a * by_row[m : m + 1] for m in range(members)], axis=0)
            deep = wide_b // nk
            for k in far + [0]:
                place = lax.rem(place_z + k, nk)
                rows = pl.ds(pl.multiple_of(place * deep, 8), deep)
                out_b[:, place] = dot(tensor_t[rows, :], weighted).reshape(4, -1, rank)
                scatter_near(32, out_b, near_b, place)
            for k in range(nk):
                over(32 + k, near_b, pl.ds(0, 3), 0)
            arrived(10)
            gram_start(1, dot(ring_m[...].reshape(nz * 8, rank), inverse[...]), False)
            for k in far + [0]:
                place = lax.rem(place_z + k, nk)
                arrived(32, place)
                part_b[place] = (out_b[class_z, place] + near_b[0, place]) + (near_b[1, place] + near_b[2, place])
                if k:
                    scatter_far(13, part_b, far_b, k)
            if nk > 1:
                over(13, far_b, pl.ds(0, nk - 1))
            for m in range(members):
                contracted[m] = dot(tensor_t[:, m * wide_a : (m + 1) * wide_a], whole_a)
            rows_a[...] = dot(rows_m[...], inverse[...])
            gram_middle(1, False)
            arrived(13)
            total = part_b[place_z]
            for k in range(nk - 1):
                total = total + far_b[k]
            rows_b[...] = total
            gather_start(25, rows_b, (block_b, 1))
            gram = leading(1)
            across, along = scales(gram, wide_a * nz)
            half[...] = gram / (across * along) * gram_c[0:128, 0:128]

        @pl.when(i == 3)
        def _():
            gram = gram_of(1)
            across, along = scales(gram, wide_a * nz)
            scale_a[...] = across
            gram_a = gram / (across * along)
            system[...] = gram_a * gram_c[...]
            gram_c[...] = gram_a
            own = rows_a[...] / across
            new_a[...] = jnp.where(core == 0, own[0:4], own[4:8])
            gather_on(25, (block_b, 1))

        @pl.when(i == 4)
        def _():
            per_scale_a = 1.0 / scale_a[...]
            for m in range(members):
                contracted[m] = contracted[m] * per_scale_a
            raw_b_own[...] = dot(rows_b[...] * per_scale_a, inverse[...])
            gather_end(25)

            raw_b = dot(gathered(block_b.at[1]) * per_scale_a, inverse[...])
            gram_start(2, raw_b, True)
            sums = jnp.concatenate(
                [jnp.sum(contracted[m] * raw_b, axis=0, keepdims=True) for m in range(members)], axis=0
            )
            out_c[0] = sums[:, 0:128]
            out_c[1] = sums[:, 128:256]
            send_c(16, out_c, in_c, lambda other: other % 2)
            gram_middle(2, True)
            arrived(16)
            half_c[...] = sum_of(in_c)
            send_all_z(17, half_c, ring_c)
            gram = leading(2)
            across, along = scales(gram, wide_b * nc)
            half[...] = gram_c[0:128, 0:128] * (gram / (across * along))

        @pl.when(i == 5)
        def _():
            gram = gram_of(2)
            across, along = scales(gram, wide_b * nc)
            scale_b[...] = across
            system[...] = gram_c[...] * (gram / (across * along))
            new_b[...] = raw_b_own[...] / across
            arrived(17)
            side_c[core] = sum_of(ring_c)
            copy(15, side_c.at[core], side_c.at[core], (z, c + 1 - 2 * core)).start()
            over(15, side_c, 0)

        @pl.when(i % 2 == 1)
        def _():
            between_halves(system, half, first, right, down)

        invert_half(half)
        return carry

    lax.fori_loop(0, 6, stage, 0)
    after_halves(half, first, right, down, inverse)
    arrived(15)
    new_c[...] = dot(jnp.concatenate([side_c[0], side_c[1]], axis=1) / scale_b[...], inverse[...])
    for which in totals:
        left(which)


def solution(mesh):
    nz, nc = mesh.shape["row"], mesh.shape["col"]
    nq, nk = nc // 2, nz // 4

    def on_device(tensor, factor_b, factor_c):
        members, wide_a, wide_b = tensor.shape
        deep_b, rank = factor_b.shape
        part = rank // nc
        memory = [
            tensor.shape,
            factor_b.shape,
            factor_c.shape,
            (wide_b, members * wide_a),
            (rank, rank),
            (2, 4, nk, deep_b, rank),
            (3, 2, nc, part, 128),
            (3, 2, nc, part, 128),
            (3, 2, part, 128),
            (3, 2, nc, part, 128),
            (nq, 8, rank),
            (nc, 8, rank),
            (8, rank),
            (8, rank),
            (nz, 8, rank),
            (nq, 8, rank),
            (members, wide_b, rank),
            (4, nk, deep_b, rank),
            (3, nk, deep_b, rank),
            (nk, deep_b, rank),
            (max(nk - 1, 1), deep_b, rank),
            (deep_b, rank),
            (deep_b, rank),
            (2, members, 128),
            (nc, members, 128),
            (members, 128),
            (nz, members, 128),
            (2, members, 128),
            (rank, rank),
            (128, 128),
            (128, 128),
            (128, 128),
            (128, 128),
            (rank, rank),
            (1, rank),
            (1, rank),
        ]
        return pl.pallas_call(
            functools.partial(sweep, nz, nc),
            out_shape=(
                jax.ShapeDtypeStruct((wide_a // nc, rank), f32),
                jax.ShapeDtypeStruct((deep_b, rank), f32),
                jax.ShapeDtypeStruct((members, rank), f32),
            ),
            in_specs=[pl.BlockSpec(memory_space=pltpu.HBM)] * 3,
            out_specs=tuple([pl.BlockSpec(memory_space=pltpu.VMEM)] * 3),
            scratch_shapes=[pltpu.VMEM(shape, f32) for shape in memory]
            + [pltpu.SemaphoreType.DMA((EXCHANGES,)), pltpu.SemaphoreType.DMA((EXCHANGES,))]
            + [pltpu.SemaphoreType.DMA((3,))],
            compiler_params=pltpu.CompilerParams(
                collective_id=0, has_side_effects=True, vmem_limit_bytes=64 * 1024 * 1024 - 524288
            ),
        )(tensor, factor_b, factor_c)

    return jax.shard_map(
        on_device,
        mesh=mesh,
        in_specs=(P(None, "row", "col"), P("row", "col"), P()),
        out_specs=(P(("row", "col"), None), P("row", "col"), P()),
        check_vma=False,
    )
```
